256 devices in a mesh: tile: 64 (over x, z_hi, y, core), vis: 4 (over z_lo).
Axes of the slice: x: 4, y: 4, z: 8 (z_hi: 2, z_lo: 4; z = z_hi * 4 + z_lo), core: 2. Of those that a mesh axis runs over, the one named last changes fastest.
Arguments:
- model_image: float32 [512, 32768], P(('tile', 'vis')), may hold values from -1.2 to 1.2
- psf: float32 [512, 512], P(('tile', 'vis')), may hold values from -1 to 2
- kernel_table: float32 [128, 8], replicated, may hold values from 0.1 to 1
- observed: float32 [2, 4, 1024, 256], P(None, 'vis', 'tile'), may hold values from -3.6 to 3.6
- visit_tile: int32 [4, 1024], P('vis', 'tile'), may hold values from 0 to 15, as said below
- visit_count: int32 [4, 1024], P('vis', 'tile'), may hold values from 1 to 256, as said below
- cell_offset: int32 [2, 4, 1024, 256], P(None, 'vis', 'tile'), may hold values from 0 to 120
- kernel_row: int32 [2, 4, 1024, 256], P(None, 'vis', 'tile'), may hold values from 0 to 127
Outputs:
- model_next: float32 [512, 32768], P(('tile', 'vis'))
- residual_image: float32 [512, 32768], P(('tile', 'vis'))
The draws below stay inside these ranges and needn't reach their ends.
Inputs may be any that keep to these rules, and one draw needn't show every extreme that they name: `visit_tile`: within the 16 visits of one tile index (positions along the second dimension in blocks of 16), visit j lies in one of the 4 tiles numbered from k * 4 on, k = j // 4. `visit_count`: slots below the count hold visibilities; the others are dead.
All inputs are finite; a program needn't handle non-finite values.
Results may differ from the reference program's by a relative error of at most 0.0051.
Values may be sent and summed in bfloat16 or wider, within the bound.
No kernel may reach another device: no remote copies, remote signals or barrier semaphores. Data moves between devices by JAX's collectives and lax.ppermute only.
A program may use at most 64 MiB of HBM per device.

```python
import jax
import jax.numpy as jnp
from jax import lax

GU = 32768
GV = 512
UVT = 128
KS = 8
KROWS = 128
CAP = 256
VISITS = 16
ITERS = 3
TILES_SUB = 4
VISITS_ALL = 1024
N_TILE = 64
N_VIS = 4


def draw_visit_tile(key, part):
    key = jax.random.fold_in(key, 11)
    group = VISITS // N_VIS
    local = jnp.arange(VISITS_ALL) % VISITS
    block = local // group * TILES_SUB
    pick = jax.random.randint(key, (N_VIS, VISITS_ALL), 0, TILES_SUB)
    return (block[None, :] + pick).astype(jnp.int32)


def draw_visit_count(key, part):
    key = jax.random.fold_in(key, 12)
    key_load, key_base, key_full = jax.random.split(key, 3)
    load = jax.random.randint(key_load, (N_VIS, N_TILE), 2, 5)
    base = jax.random.randint(key_base, (N_VIS, VISITS_ALL), CAP // 4, CAP + 1)
    scaled = jnp.maximum(1, base * jnp.repeat(load, VISITS, axis=1) // 4)
    full = jax.random.randint(key_full, (N_VIS, 1), 0, VISITS_ALL)
    counts = jnp.where(jnp.arange(VISITS_ALL)[None, :] == full, CAP, scaled)
    return counts.astype(jnp.int32)


def draw_psf(key, part):
    key = jax.random.fold_in(key, 13)
    sidelobes = jax.random.normal(key, (GV, GV), jnp.float32) * (2.0 / GV)
    rows = jnp.arange(GV)[:, None]
    cols = jnp.arange(GV)[None, :]
    peak = jnp.where((rows == 0) & (cols == GV // 2), 1.0, 0.0).astype(jnp.float32)
    return sidelobes + peak


def with_ends(entries, key, least, top_value):
    longest = entries.shape.index(max(entries.shape))
    spots = []
    for shift in (0, 1):
        where = [jax.random.randint(jax.random.fold_in(key, axis), (), 0, length) for axis, length in enumerate(entries.shape)]
        where[longest] = (where[longest] + shift) % entries.shape[longest]
        spots.append(tuple(where))
    return entries.at[spots[0]].set(least).at[spots[1]].set(top_value)


def level_of(rng, dims, shards, low, high):
    loudness, own = 1.0, jax.random.fold_in(rng, 6)
    for axis_at, blocks in shards:
        heights = jnp.exp(jax.random.uniform(jax.random.fold_in(own, axis_at), (blocks,), jnp.float32, low / len(shards), high / len(shards)))
        loudness = loudness * jnp.repeat(heights, dims[axis_at] // blocks).reshape([-1 if axis == axis_at else 1 for axis in range(len(dims))])
    return loudness


def gaussian(own_key, shape, deviation, limit, shards=(), kind=jnp.bfloat16):
    result = jax.random.normal(own_key, shape, jnp.float32) * deviation
    if len(shards) > 0:
        result = level_of(own_key, shape, shards, -0.22, 0.18) * result
    return jnp.clip(result, min=-limit, max=limit).astype(kind)


def setup_inputs(seed: int = 0) -> dict:
    streams_of = jax.random.split(jax.random.key(seed), 9)
    return {
        "model_image": gaussian(streams_of[0], (GV, GU), 0.2, 1.2, ((0, 256),), jnp.float32),
        "psf": draw_psf(jax.random.fold_in(streams_of[8], 71), 0),
        "kernel_table": jnp.clip(jax.random.uniform(streams_of[2], (KROWS, KS), jnp.float32, 0.1, 1.0), 0.1, 1.0),
        "observed": gaussian(streams_of[3], (2, N_VIS, VISITS_ALL, CAP), 0.6, 3.6, ((1, 4), (2, 64)), jnp.float32),
        "visit_tile": draw_visit_tile(jax.random.fold_in(streams_of[8], 71), 0),
        "visit_count": draw_visit_count(jax.random.fold_in(streams_of[8], 71), 0),
        "cell_offset": with_ends(jax.random.randint(streams_of[6], (2, N_VIS, VISITS_ALL, CAP), 0, UVT - KS + 1), jax.random.fold_in(streams_of[6], 1), 0, UVT - KS).astype(jnp.int32),
        "kernel_row": with_ends(jax.random.randint(streams_of[7], (2, N_VIS, VISITS_ALL, CAP), 0, KROWS), jax.random.fold_in(streams_of[7], 1), 0, KROWS - 1).astype(jnp.int32),
    }


STEP_SIZE = 0.5
THRESHOLD = 0.05


def residual_region(grid_real, grid_imag, table, observed, visit_tile, visit_count, cell_offset, kernel_row):
    tile_rows = GV // UVT
    width = grid_real.shape[1]
    row_start = (visit_tile % tile_rows) * UVT
    col_start = (visit_tile // tile_rows) * UVT
    rows = row_start[..., None] + cell_offset[0]
    cols = col_start[..., None] + cell_offset[1]
    taps_row = table[kernel_row[0]].astype(jnp.float32)
    taps_col = table[kernel_row[1]].astype(jnp.float32)
    live = (jnp.arange(CAP)[None, None, :] < visit_count[..., None]).astype(jnp.float32)
    offsets = jnp.arange(KS)
    cell_rows = rows[..., None, None] + offsets[:, None]
    cell_cols = cols[..., None, None] + offsets[None, :]
    weights = taps_row[..., :, None] * taps_col[..., None, :]
    model_real = jnp.sum(weights * grid_real[cell_rows, cell_cols].astype(jnp.float32), axis=(-2, -1))
    model_imag = jnp.sum(weights * grid_imag[cell_rows, cell_cols].astype(jnp.float32), axis=(-2, -1))
    resid_real = live * (observed[0] - model_real)
    resid_imag = live * (observed[1] - model_imag)
    spread_real = lax.optimization_barrier((resid_real[..., None] * taps_col).astype(jnp.bfloat16)).astype(jnp.float32)
    spread_imag = lax.optimization_barrier((resid_imag[..., None] * taps_col).astype(jnp.bfloat16)).astype(jnp.float32)
    update_real = taps_row[..., :, None] * spread_real[..., None, :]
    update_imag = taps_row[..., :, None] * spread_imag[..., None, :]
    empty = jnp.zeros((GV, width), jnp.float32)
    out_real = empty.at[cell_rows, cell_cols].add(update_real)
    out_imag = empty.at[cell_rows, cell_cols].add(update_imag)
    return out_real, out_imag


def reference(model_image, psf, kernel_table, observed, visit_tile, visit_count, cell_offset, kernel_row):
    model_grid = jnp.fft.fft2(model_image, norm="ortho")
    grid_real = jnp.real(model_grid).astype(jnp.bfloat16)
    grid_imag = jnp.imag(model_grid).astype(jnp.bfloat16)
    table = kernel_table.astype(jnp.bfloat16)
    width = GU // N_TILE

    def one_device(index):
        start = (index * width).astype(jnp.int32)
        region_real = lax.dynamic_slice_in_dim(grid_real, start, width, 1)
        region_imag = lax.dynamic_slice_in_dim(grid_imag, start, width, 1)
        first = (index * VISITS).astype(jnp.int32)
        tiles_here = lax.dynamic_slice_in_dim(visit_tile, first, VISITS, 1)
        counts_here = lax.dynamic_slice_in_dim(visit_count, first, VISITS, 1)
        observed_here = lax.dynamic_slice_in_dim(observed, first, VISITS, 2)
        offsets_here = lax.dynamic_slice_in_dim(cell_offset, first, VISITS, 2)
        kernels_here = lax.dynamic_slice_in_dim(kernel_row, first, VISITS, 2)
        return residual_region(region_real, region_imag, table, observed_here, tiles_here, counts_here, offsets_here, kernels_here)

    parts_real, parts_imag = lax.map(one_device, jnp.arange(N_TILE, dtype=jnp.int32))
    res_real = jnp.transpose(parts_real, (1, 0, 2)).reshape(GV, GU)
    res_imag = jnp.transpose(parts_imag, (1, 0, 2)).reshape(GV, GU)
    residual_grid = res_real + 1j * res_imag
    residual_image = jnp.real(jnp.fft.ifft2(residual_grid, norm="ortho"))
    padded = jnp.concatenate([psf[:, GV // 2:], jnp.zeros((GV, GU - GV), psf.dtype), psf[:, :GV // 2]], axis=1)
    transfer = jnp.fft.fft2(padded)
    model_now = model_image
    for step in range(ITERS):
        blurred = jnp.real(jnp.fft.ifft2(jnp.fft.fft2(model_now - model_image) * transfer))
        moved = model_now + STEP_SIZE * (residual_image - blurred)
        model_now = moved - jnp.clip(moved, -THRESHOLD, THRESHOLD)
    return model_now, residual_image
```

```python
import functools
import math

import jax
import jax.numpy as jnp
import numpy as np
from jax import lax
from jax.experimental import pallas as pl
from jax.experimental.pallas import tpu as pltpu
from jax.sharding import PartitionSpec as P

GU = 32768
GV = 512
UVT = 128
CAP = 256
N_TILE = 64
N_VIS = 4
BLOCKS = N_TILE * N_VIS
WIDTH = GU // BLOCKS
HALO = 640
PHASES = 3
STEP_SIZE = 0.5
THRESHOLD = 0.05
JOINT = ("tile", "vis")
F32 = jnp.float32
BF16 = jnp.bfloat16
NN = (((1,), (0,)), ((), ()))
NT = (((1,), (1,)), ((), ()))
TN = (((0,), (0,)), ((), ()))
MIB = 1024 * 1024


def angles(left, right, length):
    return 2.0 * math.pi / length * ((np.asarray(left)[:, None] * np.asarray(right)[None, :]) % length)


def split_table(table, axis):
    table = np.asarray(table, np.float32)
    high = table.astype(jnp.bfloat16)
    low = (table - high.astype(np.float32)).astype(jnp.bfloat16)
    return np.concatenate([high, low], axis)


def block_owner():
    owner = []
    for run in range(16):
        x, y = run // 4, run % 4
        y = y if x % 2 == 0 else 3 - y
        for spot in range(8):
            z = spot if run % 2 == 0 else 7 - spot
            for core in range(2):
                owner.append((((x * 2 + z // 4) * 4 + y) * 2 + core) * 4 + z % 4)
    return owner


def build_tables():
    tables = {}
    scale = 1.0 / math.sqrt(GV * GU)
    first = angles(np.arange(256), np.arange(256), 256)
    second = angles(np.arange(128), np.arange(128), 128)
    cosine, sine = np.cos(second), np.sin(second)
    twiddle = angles(np.arange(128), np.arange(256), GU)
    tables["row_twiddle"] = (np.stack([np.cos(twiddle), -np.sin(twiddle)]) * scale).astype(np.float32)
    half = angles([1], np.arange(128), 256)
    tables["half_twiddle"] = np.concatenate([np.cos(half), np.sin(half)]).astype(np.float32)
    tables["back_first"] = split_table(np.concatenate([np.cos(first), np.sin(first)], 0), 1)
    tables["back_twiddle"] = np.stack([np.cos(twiddle.T), np.sin(twiddle.T)]).astype(np.float32)
    tables["back_second"] = split_table(np.concatenate([cosine, -sine], 1) * scale, 1)
    block = np.block([[cosine, -sine], [sine, cosine]])
    tables["point_right"] = split_table(block, 0)
    tables["point_left"] = split_table(block.T, 1)
    tables["point_back"] = split_table(block, 1)
    quarter = angles(np.arange(4), np.arange(128), GV)
    tables["lane_twiddle"] = np.stack([np.cos(quarter), np.sin(quarter)], 1).astype(np.float32)
    rows = np.stack([np.cos(quarter[1:]), np.sin(quarter[1:])], 1)[:, :, :, None]
    tables["side_twiddle"] = np.broadcast_to(rows, (3, 2, 128, 128)).astype(np.float32)
    window = angles(np.arange(PHASES), np.arange(128), HALO)
    tables["window_twiddle"] = np.stack([np.cos(window), np.sin(window)], 1).astype(np.float32)
    back = []
    for phase in range(PHASES):
        share = (1.0 if phase == 0 else 2.0) / (GV * HALO)
        turn = angles(5 * np.arange(128) + phase, 256 + np.arange(128), HALO)
        back.append(split_table(np.concatenate([np.cos(turn), -np.sin(turn)], 0) * share, 0))
    tables["window_back"] = np.stack(back)
    return tables


TABLES = build_tables()
OWNER = block_owner()


def window_turns():
    place = np.array([3, 4, 0, 1])
    out = np.zeros((N_VIS, PHASES, N_VIS, 2), np.float32)
    for at in range(N_VIS):
        for phase in range(PHASES):
            for block in range(N_VIS):
                turn = 2.0 * math.pi * (place[(at + block) % N_VIS] * phase % 5) / 5.0
                out[at, phase, block] = (math.cos(turn), math.sin(turn))
    return out.reshape(N_VIS, -1)


def dot(left, right, dims=NN):
    return lax.dot_general(left, right, dims, preferred_element_type=F32)


def parts(value, axis):
    high = value.astype(BF16)
    low = (value - high.astype(F32)).astype(BF16)
    return jnp.concatenate([high, low, high], axis=axis)


def both(table, axis):
    high, low = jnp.split(table[...], 2, axis=axis)
    return jnp.concatenate([high, high, low], axis=axis)


def twice(value, axis):
    return jnp.concatenate([value, value], axis=axis)


def call(kernel, outs, *args, smem=(), scratch=(), flops=0, vmem=32):
    specs = [
        pl.BlockSpec(memory_space=pltpu.SMEM if at in smem else pltpu.VMEM) for at in range(len(args))
    ]
    size = sum(int(np.prod(a.shape)) * a.dtype.itemsize for a in args)
    size += sum(int(np.prod(o.shape)) * o.dtype.itemsize for o in outs)
    return pl.pallas_call(
        kernel,
        out_shape=outs,
        in_specs=specs,
        out_specs=[pl.BlockSpec(memory_space=pltpu.VMEM)] * len(outs),
        scratch_shapes=list(scratch),
        compiler_params=pltpu.CompilerParams(vmem_limit_bytes=vmem * MIB),
        cost_estimate=pl.CostEstimate(flops=flops, bytes_accessed=size, transcendentals=0),
    )(*args)


def shape(dims, dtype):
    return jax.ShapeDtypeStruct(dims, dtype)


def cross_forward(blocks):
    (r0, i0), (r1, i1), (r2, i2), (r3, i3) = blocks
    ar, ai, br, bi = r0 + r2, i0 + i2, r0 - r2, i0 - i2
    cr, ci, dr, di = r1 + r3, i1 + i3, r1 - r3, i1 - i3
    return [(ar + cr, ai + ci), (br + di, bi - dr), (ar - cr, ai - ci), (br - di, bi + dr)]


def cross_back(blocks):
    (r0, i0), (r1, i1), (r2, i2), (r3, i3) = blocks
    ar, ai, br, bi = r0 + r2, i0 + i2, r0 - r2, i0 - i2
    cr, ci, dr, di = r1 + r3, i1 + i3, r1 - r3, i1 - i3
    return [(ar + cr, ai + ci), (br - di, bi + dr), (ar - cr, ai - ci), (br + di, bi - dr)]


def turn_forward(real, imag, cosine, sine):
    return real * cosine + imag * sine, imag * cosine - real * sine


def turn_back(real, imag, cosine, sine):
    return real * cosine - imag * sine, imag * cosine + real * sine


def row_kernel(sky_ref, psf_ref, right, half_turn, twiddle, left, out_ref, lines, send):
    for at in range(BLOCKS):
        piece = sky_ref[:, at * 128 : at * 128 + 128]
        lines[2 * at : 2 * at + 2, :] = piece
        row = 8 * OWNER[at] + 4
        send[row : row + 2, :] = piece
    for at in range(N_VIS):
        piece = psf_ref[:, at * 128 : at * 128 + 128]
        for tile in range(N_TILE):
            row = 8 * (tile * N_VIS + at) + 6
            send[row : row + 2, :] = piece
    pieces = [
        lines[pl.ds(2 * odd + row, 128, stride=4), :] for row in range(2) for odd in range(2)
    ]
    high, low = right[0:128, :], right[256:384, :]
    mixed = dot(parts(jnp.concatenate(pieces, 1), 0), jnp.concatenate([high, high, low], 0), TN)
    for row in range(2):
        even = mixed[row * 256 : row * 256 + 128]
        odd = mixed[row * 256 + 128 : row * 256 + 256]
        odd_real, odd_imag = turn_forward(odd[:, :128], odd[:, 128:], half_turn[0:1], half_turn[1:2])
        real = jnp.concatenate([even[:, :128] + odd_real, even[:, :128] - odd_real], axis=1)
        imag = jnp.concatenate([even[:, 128:] + odd_imag, even[:, 128:] - odd_imag], axis=1)
        turned = jnp.concatenate(
            [real * twiddle[0] - imag * twiddle[1], real * twiddle[1] + imag * twiddle[0]], axis=0
        )
        done = dot(both(left, 1), parts(turned, 0))
        for half in range(2):
            send[pl.ds(8 * half + row, 128, stride=16), :] = done[:128, half * 128 : half * 128 + 128]
            send[pl.ds(8 * half + 2 + row, 128, stride=16), :] = done[128:, half * 128 : half * 128 + 128]
    out_ref[...] = send[...].astype(BF16)


def weight_kernel(taps_ref, visit_ref, row_ref, col_ref):
    taps_table = taps_ref[...]
    place = lax.broadcasted_iota(jnp.int32, (UVT, CAP), 0).astype(F32)

    def weights(offset, row):
        choose = jnp.where(place == row, 1.0, 0.0).astype(BF16)
        taps = dot(taps_table, choose)
        within = place - offset
        out = jnp.zeros((UVT, CAP), F32)
        for shift in range(8):
            out = jnp.where(within == float(shift), taps[shift : shift + 1, :], out)
        return out.astype(BF16)

    def pair(group, carry):
        for side in range(2):
            at = 2 * group + side
            entry = visit_ref[at]
            row_ref[at] = weights(entry[2:3], entry[4:5])
            col_ref[at] = weights(entry[3:4], entry[5:6])
        return carry

    lax.fori_loop(0, visit_ref.shape[0] // 2, pair, 0)


def uv_kernel(
    tile_ref, got_ref, visit_ref, row_ref, col_ref, right, back, twiddle, out_ref, base_ref, psf_ref,
    move, grid, resid, side,
):
    move[...] = got_ref[...].astype(F32)
    for slot, ref in ((4, base_ref), (6, psf_ref)):
        for row in range(2):
            side[pl.ds(row, 256, stride=2), :] = move[pl.ds(slot + row, 256, stride=8), :]
        ref[...] = side[...].astype(BF16)
    lines = []
    for rho in range(4):
        row = 8 * (rho // 2) + rho % 2
        lines.append(
            jnp.concatenate(
                [move[pl.ds(row, 128, stride=16), :], move[pl.ds(row + 2, 128, stride=16), :]], 0
            )
        )
    lines = jnp.concatenate(lines, axis=1).astype(BF16)
    mixed = dot(twice(lines, 0), right[...], TN)
    blocks = []
    for rho in range(4):
        real, imag = mixed[rho * 128 : rho * 128 + 128, :128], mixed[rho * 128 : rho * 128 + 128, 128:]
        if rho > 0:
            real, imag = turn_forward(real, imag, twiddle[rho, 0:1], twiddle[rho, 1:2])
        blocks.append((real, imag))
    for at, (real, imag) in enumerate(cross_forward(blocks)):
        grid[0:128, at * 128 : at * 128 + 128] = real.astype(BF16)
        grid[128:256, at * 128 : at * 128 + 128] = imag.astype(BF16)
    resid[...] = jnp.zeros_like(resid)

    def some(group, carry):
        for side in range(4):
            at = 4 * group + side
            start = pl.multiple_of(tile_ref[at] * UVT, UVT)
            entry = visit_ref[at]
            weight_row = row_ref[at]
            weight_col = col_ref[at].astype(F32)
            partial = dot(grid[:, pl.ds(start, UVT)], weight_row)
            model_real = jnp.sum(partial[:UVT] * weight_col, axis=0, keepdims=True)
            model_imag = jnp.sum(partial[UVT:] * weight_col, axis=0, keepdims=True)
            live = entry[6:7] > 0.5
            real = jnp.where(live, entry[0:1] - model_real, 0.0)
            imag = jnp.where(live, entry[1:2] - model_imag, 0.0)
            spread = jnp.concatenate([real * weight_col, imag * weight_col], axis=0).astype(BF16)
            resid[:, pl.ds(start, UVT)] += dot(spread, weight_row, NT)
        return carry

    lax.fori_loop(0, visit_ref.shape[0] // 4, some, 0)
    blocks = [
        (resid[0:128, at * 128 : at * 128 + 128], resid[128:256, at * 128 : at * 128 + 128])
        for at in range(4)
    ]
    turned = []
    for rho, (real, imag) in enumerate(cross_back(blocks)):
        if rho > 0:
            real, imag = turn_back(real, imag, twiddle[rho, 0:1], twiddle[rho, 1:2])
        turned.append(jnp.concatenate([real, imag], axis=1))
    done = dot(both(back, 1), parts(jnp.concatenate(turned, axis=0), 1), NT)
    for rho in range(4):
        row = 4 * (rho // 2) + rho % 2
        move[pl.ds(row, 128, stride=8), :] = done[:128, rho * 128 : rho * 128 + 128]
        move[pl.ds(row + 2, 128, stride=8), :] = done[128:, rho * 128 : rho * 128 + 128]
    out_ref[...] = move[0:1024, :].astype(BF16)


def back_kernel(got_ref, first, twiddle, second, out_ref, send_ref, move, send):
    move[...] = got_ref[...].astype(F32)
    lines = jnp.concatenate([move[pl.ds(slot, 256, stride=4), :] for slot in range(4)], 1).astype(BF16)
    mixed = dot(first[...], twice(lines, 0))
    for row in range(2):
        at = row * 128
        real = mixed[:256, at : at + 128] - mixed[256:, 256 + at : 384 + at]
        imag = mixed[256:, at : at + 128] + mixed[:256, 256 + at : 384 + at]
        turned = jnp.concatenate(
            [real * twiddle[0] - imag * twiddle[1], real * twiddle[1] + imag * twiddle[0]], axis=1
        )
        done = dot(both(second, 1), parts(turned, 1), NT)
        for half in range(2):
            move[pl.ds(2 * half + row, 128, stride=4), :] = done[:, half * 128 : half * 128 + 128]
    for at in range(BLOCKS):
        piece = move[2 * at : 2 * at + 2, :]
        out_ref[:, at * 128 : at * 128 + 128] = piece
        send[2 * OWNER[at] : 2 * OWNER[at] + 2, :] = piece
    send_ref[...] = send[...].astype(BF16)


def gather_window(blocks, phase):
    real, imag = None, None
    for at, value in enumerate(blocks):
        angle = 2.0 * math.pi * (at * phase % 5) / 5.0
        term = value * math.cos(angle) if at * phase % 5 else value
        real = term if real is None else real + term
        if at * phase % 5:
            term = value * -math.sin(angle)
            imag = term if imag is None else imag + term
    return real, imag


def to_frequency(real, imag, phase, window, side, right, left):
    if phase == 0:
        lines = parts(real, 1)
        table = jnp.concatenate([right[0:128, :], right[0:128, :], right[256:384, :]], axis=0)
    else:
        real, imag = turn_forward(real, imag, window[phase, 0:1], window[phase, 1:2])
        lines = parts(jnp.concatenate([real, imag], axis=1), 1)
        table = both(right, 0)
    mixed = dot(lines, table)
    quarters = [
        (mixed[at * 128 : at * 128 + 128, :128], mixed[at * 128 : at * 128 + 128, 128:])
        for at in range(4)
    ]
    turned = []
    for at, (real, imag) in enumerate(cross_forward(quarters)):
        if at > 0:
            real, imag = turn_forward(real, imag, side[at - 1, 0], side[at - 1, 1])
        turned.append(jnp.concatenate([real, imag], axis=0))
    done = dot(both(left, 1), parts(jnp.concatenate(turned, axis=1), 0))
    return done[:128], done[128:]


def transfer_kernel(turn_ref, *refs):
    blocks = [ref[...].astype(F32) for ref in refs[:N_VIS]]
    window, side, right, left, out_ref = refs[N_VIS:]
    for phase in range(PHASES):
        real, imag = None, None
        for at, value in enumerate(blocks):
            place = 2 * (phase * N_VIS + at)
            term = value * turn_ref[place] if phase else value
            real = term if real is None else real + term
            if phase:
                term = value * turn_ref[place + 1]
                imag = -term if imag is None else imag - term
        out_ref[phase, 0], out_ref[phase, 1] = to_frequency(
            real, imag, phase, window, side, right, left
        )


def conv_kernel(
    first, far_left, near_left, own, near_right, far_right, transfer, window, side, right, left,
    back, window_back, sky_ref, resid_ref, base_ref, *out_refs,
):
    blocks = [
        ref[...].astype(F32) for ref in (far_left, near_left, own, near_right, far_right)
    ]
    total = jnp.zeros((GV, 128), F32)
    for phase in range(PHASES):
        real, imag = gather_window(blocks, phase)
        real, imag = to_frequency(real, imag, phase, window, side, right, left)
        trans_real, trans_imag = transfer[phase, 0], transfer[phase, 1]
        blur = jnp.concatenate(
            [real * trans_real - imag * trans_imag, real * trans_imag + imag * trans_real], axis=0
        )
        mixed = dot(both(back, 1), parts(blur, 0))
        quarters = []
        for at in range(4):
            real, imag = mixed[:128, at * 128 : at * 128 + 128], mixed[128:, at * 128 : at * 128 + 128]
            if at > 0:
                real, imag = turn_back(real, imag, side[at - 1, 0], side[at - 1, 1])
            quarters.append((real, imag))
        lines = [jnp.concatenate([real, imag], axis=1) for real, imag in cross_back(quarters)]
        high, low = window_back[phase, 0:256], window_back[phase, 256:512]
        table = jnp.concatenate([high, high, low], axis=0)
        total = total + dot(parts(jnp.concatenate(lines, axis=0), 1), table)
    resid = resid_ref[...].astype(F32)
    base = base_ref[...].astype(F32)
    sky = step(base, resid) if first else sky_ref[...]
    sky = step(sky, resid - total)
    if first:
        out_refs[0][...] = sky
        out_refs[1][...] = (sky - base).astype(BF16)
    else:
        out_refs[0][...] = sky.astype(BF16)


def step(sky, gradient):
    moved = sky + STEP_SIZE * gradient
    return moved - jnp.clip(moved, -THRESHOLD, THRESHOLD)


def last_kernel(got_ref, out_ref, move):
    move[...] = got_ref[...].astype(F32)
    for at in range(BLOCKS):
        out_ref[:, at * 128 : at * 128 + 128] = move[2 * OWNER[at] : 2 * OWNER[at] + 2, :]


def exchange(rows):
    blocks = rows.reshape(BLOCKS, rows.shape[0] // BLOCKS, 128)
    return lax.all_to_all(blocks, JOINT, 0, 0, tiled=True).reshape(rows.shape)


def halo(block, step):
    pairs = [(OWNER[at], OWNER[(at + step) % BLOCKS]) for at in range(BLOCKS)]
    return lax.ppermute(block, JOINT, pairs)


def around_vis(value, step):
    return lax.ppermute(value, "vis", [(at, (at + step) % N_VIS) for at in range(N_VIS)])


def shards(
    model_image, psf, kernel_table, observed, visit_tile, visit_count, cell_offset, kernel_row
):
    at_vis = lax.axis_index("vis")
    tables = TABLES

    live = jnp.arange(CAP)[None, :] < visit_count[0][:, None]
    tile_row = jnp.broadcast_to((visit_tile[0] % 4)[:, None], live.shape)
    packed = jnp.stack(
        [
            observed[0, 0],
            observed[1, 0],
            cell_offset[0, 0].astype(F32),
            cell_offset[1, 0].astype(F32),
            kernel_row[0, 0].astype(F32),
            kernel_row[1, 0].astype(F32),
            live.astype(F32),
            tile_row.astype(F32),
        ],
        axis=1,
    )
    pieces = [lax.dynamic_slice_in_dim(packed, at_vis * 4, 4, 0)]
    for hop in range(1, N_VIS):
        group = lax.dynamic_slice_in_dim(packed, (at_vis + hop) % N_VIS * 4, 4, 0)
        pieces.append(around_vis(group, hop))
    visits = jnp.concatenate(pieces, axis=0)

    send = call(
        row_kernel,
        [shape((8 * BLOCKS, 128), BF16)],
        model_image,
        psf,
        tables["point_right"],
        tables["half_twiddle"],
        tables["row_twiddle"],
        tables["point_left"],
        vmem=60,
        scratch=[pltpu.VMEM((512, 128), F32), pltpu.VMEM((8 * BLOCKS, 128), F32)],
        flops=2 * 3 * 256 * 256 * 1024,
    )[0]
    got = exchange(send)
    visit_rows = visits[:, 7, 0].astype(jnp.int32)
    taps = jnp.pad(kernel_table.astype(BF16).T, ((0, 8), (0, 0)))
    weight_row, weight_col = call(
        weight_kernel,
        [shape((16, UVT, CAP), BF16), shape((16, UVT, CAP), BF16)],
        taps,
        visits,
        flops=2 * 16 * 2 * 16 * 128 * 256 * 64,
    )

    send, base, quarter = call(
        uv_kernel,
        [shape((4 * BLOCKS, 128), BF16), shape((GV, 128), BF16), shape((GV, 128), BF16)],
        visit_rows,
        got,
        visits,
        weight_row,
        weight_col,
        tables["point_right"],
        tables["point_back"],
        tables["lane_twiddle"],
        smem=(0,),
        scratch=[
            pltpu.VMEM((8 * BLOCKS, 128), F32),
            pltpu.VMEM((256, GV), BF16),
            pltpu.VMEM((256, GV), F32),
            pltpu.VMEM((GV, 128), F32),
        ],
        flops=2 * 7 * 256 * 512 * 512,
    )
    got = exchange(send)
    transfer = call(
        transfer_kernel,
        [shape((PHASES, 2, 128, 4 * 128), F32)],
        lax.dynamic_index_in_dim(jnp.asarray(window_turns()), at_vis, 0, keepdims=False),
        quarter,
        *[around_vis(quarter, N_VIS - hop) for hop in range(1, N_VIS)],
        tables["window_twiddle"],
        tables["side_twiddle"],
        tables["point_right"],
        tables["point_left"],
        smem=(0,),
        flops=2 * PHASES * 3 * 2 * 512 * 256 * 256,
    )[0]
    residual_image, send = call(
        back_kernel,
        [shape((2, GU), F32), shape((2 * BLOCKS, 128), BF16)],
        got,
        tables["back_first"],
        tables["back_twiddle"],
        tables["back_second"],
        scratch=[pltpu.VMEM((4 * BLOCKS, 128), F32), pltpu.VMEM((2 * BLOCKS, 128), F32)],
        flops=2 * 3 * 512 * 512 * 256,
    )

    resid = exchange(send)
    wide = base.astype(F32)
    change = (step(wide, resid.astype(F32)) - wide).astype(BF16)
    sky = wide
    for turn in range(2):
        first = turn == 0
        outs = [shape((GV, 128), F32), shape((GV, 128), BF16)] if first else [shape((GV, 128), BF16)]
        got = call(
            functools.partial(conv_kernel, first),
            outs,
            halo(change, 2),
            halo(change, 1),
            change,
            halo(change, -1),
            halo(change, -2),
            transfer,
            tables["window_twiddle"],
            tables["side_twiddle"],
            tables["point_right"],
            tables["point_left"],
            tables["point_back"],
            tables["window_back"],
            base if first else sky,
            resid,
            base,
            flops=2 * PHASES * 3 * 4 * 512 * 256 * 256,
        )
        if first:
            sky, change = got
    got = exchange(got[0])
    model_next = call(
        last_kernel, [shape((2, GU), F32)], got, scratch=[pltpu.VMEM((2 * BLOCKS, 128), F32)]
    )[0]
    return (model_next, residual_image)


def solution(mesh):
    placed = (
        P(("tile", "vis"), None),
        P(("tile", "vis"), None),
        P(),
        P(None, "vis", "tile", None),
        P("vis", "tile"),
        P("vis", "tile"),
        P(None, "vis", "tile", None),
        P(None, "vis", "tile", None),
    )
    return jax.shard_map(
        shards,
        mesh=mesh,
        in_specs=placed,
        out_specs=(P(("tile", "vis"), None), P(("tile", "vis"), None)),
        check_vma=False,
    )
```

```python
import functools
import math

import jax
import jax.numpy as jnp
import numpy as np
from jax import lax
from jax.experimental import pallas as pl
from jax.experimental.pallas import tpu as pltpu
from jax.sharding import PartitionSpec as P

GU = 32768
GV = 512
UVT = 128
CAP = 256
N_TILE = 64
N_VIS = 4
BLOCKS = N_TILE * N_VIS
WIDTH = GU // BLOCKS
HALO = 640
PHASES = 3
QUARTERS = 4
STEP_SIZE = 0.5
THRESHOLD = 0.05
JOINT = ("tile", "vis")
F32 = jnp.float32
BF16 = jnp.bfloat16
NN = (((1,), (0,)), ((), ()))
NT = (((1,), (1,)), ((), ()))
TN = (((0,), (0,)), ((), ()))
MIB = 1024 * 1024


def angles(left, right, length):
    return 2.0 * math.pi / length * ((np.asarray(left)[:, None] * np.asarray(right)[None, :]) % length)


def split_table(table, axis):
    table = np.asarray(table, np.float32)
    high = table.astype(jnp.bfloat16)
    low = (table - high.astype(np.float32)).astype(jnp.bfloat16)
    return np.concatenate([high, low], axis)


def block_owner():
    owner = []
    for run in range(16):
        x, y = run // 4, run % 4
        y = y if x % 2 == 0 else 3 - y
        for spot in range(8):
            z = spot if run % 2 == 0 else 7 - spot
            for core in range(2):
                owner.append((((x * 2 + z // 4) * 4 + y) * 2 + core) * 4 + z % 4)
    return owner


def build_tables():
    tables = {}
    scale = 1.0 / math.sqrt(GV * GU)
    first = angles(np.arange(256), np.arange(256), 256)
    second = angles(np.arange(128), np.arange(128), 128)
    cosine, sine = np.cos(second), np.sin(second)
    twiddle = angles(np.arange(128), np.arange(256), GU)
    tables["row_twiddle"] = (np.stack([np.cos(twiddle), -np.sin(twiddle)]) * scale).astype(np.float32)
    half = angles([1], np.arange(128), 256)
    tables["half_twiddle"] = np.concatenate([np.cos(half), np.sin(half)]).astype(np.float32)
    tables["back_first"] = split_table(np.concatenate([np.cos(first), np.sin(first)], 0), 1)
    tables["back_twiddle"] = np.stack([np.cos(twiddle.T), np.sin(twiddle.T)]).astype(np.float32)
    tables["back_second"] = split_table(np.concatenate([cosine, -sine], 1) * scale, 1)
    block = np.block([[cosine, -sine], [sine, cosine]])
    tables["point_right"] = split_table(block, 0)
    tables["point_left"] = split_table(block.T, 1)
    tables["point_back"] = split_table(block, 1)
    quarter = angles(np.arange(4), np.arange(128), GV)
    tables["lane_twiddle"] = np.stack([np.cos(quarter), np.sin(quarter)], 1).astype(np.float32)
    rows = np.stack([np.cos(quarter[1:]), np.sin(quarter[1:])], 1)[:, :, :, None]
    tables["side_twiddle"] = np.broadcast_to(rows, (3, 2, 128, 128)).astype(np.float32)
    window = angles(np.arange(PHASES), np.arange(128), HALO)
    tables["window_twiddle"] = np.stack([np.cos(window), np.sin(window)], 1).astype(np.float32)
    back = []
    for phase in range(PHASES):
        share = (1.0 if phase == 0 else 2.0) / (GV * HALO)
        turn = angles(5 * np.arange(128) + phase, 256 + np.arange(128), HALO)
        back.append(split_table(np.concatenate([np.cos(turn), -np.sin(turn)], 0) * share, 0))
    tables["window_back"] = np.stack(back)
    return tables


TABLES = build_tables()
OWNER = block_owner()


def window_turns():
    place = np.array([3, 4, 0, 1])
    out = np.zeros((QUARTERS, PHASES, QUARTERS, 2), np.float32)
    for at in range(QUARTERS):
        for phase in range(PHASES):
            for block in range(QUARTERS):
                turn = 2.0 * math.pi * (place[(at + block) % QUARTERS] * phase % 5) / 5.0
                out[at, phase, block] = (math.cos(turn), math.sin(turn))
    return out.reshape(QUARTERS, -1)


def dot(left, right, dims=NN):
    return lax.dot_general(left, right, dims, preferred_element_type=F32)


def parts(value, axis):
    high = value.astype(BF16)
    low = (value - high.astype(F32)).astype(BF16)
    return jnp.concatenate([high, low, high], axis=axis)


def both(table, axis):
    high, low = jnp.split(table[...], 2, axis=axis)
    return jnp.concatenate([high, high, low], axis=axis)


def twice(value, axis):
    return jnp.concatenate([value, value], axis=axis)


def call(kernel, outs, *args, smem=(), scratch=(), flops=0, vmem=32):
    specs = [
        pl.BlockSpec(memory_space=pltpu.SMEM if at in smem else pltpu.VMEM) for at in range(len(args))
    ]
    size = sum(int(np.prod(a.shape)) * a.dtype.itemsize for a in args)
    size += sum(int(np.prod(o.shape)) * o.dtype.itemsize for o in outs)
    return pl.pallas_call(
        kernel,
        out_shape=outs,
        in_specs=specs,
        out_specs=[pl.BlockSpec(memory_space=pltpu.VMEM)] * len(outs),
        scratch_shapes=list(scratch),
        compiler_params=pltpu.CompilerParams(vmem_limit_bytes=vmem * MIB),
        cost_estimate=pl.CostEstimate(flops=flops, bytes_accessed=size, transcendentals=0),
    )(*args)


def shape(dims, dtype):
    return jax.ShapeDtypeStruct(dims, dtype)


def cross_forward(blocks):
    (r0, i0), (r1, i1), (r2, i2), (r3, i3) = blocks
    ar, ai, br, bi = r0 + r2, i0 + i2, r0 - r2, i0 - i2
    cr, ci, dr, di = r1 + r3, i1 + i3, r1 - r3, i1 - i3
    return [(ar + cr, ai + ci), (br + di, bi - dr), (ar - cr, ai - ci), (br - di, bi + dr)]


def cross_back(blocks):
    (r0, i0), (r1, i1), (r2, i2), (r3, i3) = blocks
    ar, ai, br, bi = r0 + r2, i0 + i2, r0 - r2, i0 - i2
    cr, ci, dr, di = r1 + r3, i1 + i3, r1 - r3, i1 - i3
    return [(ar + cr, ai + ci), (br - di, bi + dr), (ar - cr, ai - ci), (br + di, bi - dr)]


def turn_forward(real, imag, cosine, sine):
    return real * cosine + imag * sine, imag * cosine - real * sine


def turn_back(real, imag, cosine, sine):
    return real * cosine - imag * sine, imag * cosine + real * sine


def row_kernel(sky_ref, psf_ref, right, half_turn, twiddle, left, out_ref, lines, send):
    for at in range(BLOCKS):
        piece = sky_ref[:, at * 128 : at * 128 + 128]
        lines[2 * at : 2 * at + 2, :] = piece
        row = 8 * OWNER[at] + 4
        send[row : row + 2, :] = piece
    for at in range(QUARTERS):
        piece = psf_ref[:, at * 128 : at * 128 + 128]
        for device in range(BLOCKS):
            if device // 8 % QUARTERS == at:
                send[8 * device + 6 : 8 * device + 8, :] = piece
    pieces = [
        lines[pl.ds(2 * odd + row, 128, stride=4), :] for row in range(2) for odd in range(2)
    ]
    high, low = right[0:128, :], right[256:384, :]
    mixed = dot(parts(jnp.concatenate(pieces, 1), 0), jnp.concatenate([high, high, low], 0), TN)
    for row in range(2):
        even = mixed[row * 256 : row * 256 + 128]
        odd = mixed[row * 256 + 128 : row * 256 + 256]
        odd_real, odd_imag = turn_forward(odd[:, :128], odd[:, 128:], half_turn[0:1], half_turn[1:2])
        real = jnp.concatenate([even[:, :128] + odd_real, even[:, :128] - odd_real], axis=1)
        imag = jnp.concatenate([even[:, 128:] + odd_imag, even[:, 128:] - odd_imag], axis=1)
        turned = jnp.concatenate(
            [real * twiddle[0] - imag * twiddle[1], real * twiddle[1] + imag * twiddle[0]], axis=0
        )
        done = dot(both(left, 1), parts(turned, 0))
        for half in range(2):
            send[pl.ds(8 * half + row, 128, stride=16), :] = done[:128, half * 128 : half * 128 + 128]
            send[pl.ds(8 * half + 2 + row, 128, stride=16), :] = done[128:, half * 128 : half * 128 + 128]
    out_ref[...] = send[...].astype(BF16)


def spread_taps(taps_table, offset, row, place):
    choose = jnp.where(place == row, 1.0, 0.0).astype(BF16)
    taps = dot(taps_table, choose)
    turn = (place[0:8].astype(jnp.int32) - offset.astype(jnp.int32)) & 7
    turned = jnp.zeros((8, CAP), F32)
    for shift in range(8):
        turned = jnp.where(turn == shift, taps[shift : shift + 1, :], turned)
    within = place - offset
    keep = jnp.abs(within - 3.5) < 4.0
    return jnp.where(keep, jnp.concatenate([turned] * (UVT // 8), axis=0), 0.0)


def uv_kernel(
    tile_ref, got_ref, visit_ref, taps_ref, right, back, twiddle, out_ref, base_ref, psf_ref,
    move, grid, resid, side,
):
    move[...] = got_ref[...].astype(F32)
    for slot, ref in ((4, base_ref), (6, psf_ref)):
        for row in range(2):
            side[pl.ds(row, 256, stride=2), :] = move[pl.ds(slot + row, 256, stride=8), :]
        ref[...] = side[...].astype(BF16)
    lines = []
    for rho in range(4):
        row = 8 * (rho // 2) + rho % 2
        lines.append(
            jnp.concatenate(
                [move[pl.ds(row, 128, stride=16), :], move[pl.ds(row + 2, 128, stride=16), :]], 0
            )
        )
    lines = jnp.concatenate(lines, axis=1).astype(BF16)
    mixed = dot(twice(lines, 0), right[...], TN)
    blocks = []
    for rho in range(4):
        real, imag = mixed[rho * 128 : rho * 128 + 128, :128], mixed[rho * 128 : rho * 128 + 128, 128:]
        if rho > 0:
            real, imag = turn_forward(real, imag, twiddle[rho, 0:1], twiddle[rho, 1:2])
        blocks.append((real, imag))
    for at, (real, imag) in enumerate(cross_forward(blocks)):
        grid[0:128, at * 128 : at * 128 + 128] = real.astype(BF16)
        grid[128:256, at * 128 : at * 128 + 128] = imag.astype(BF16)
    resid[...] = jnp.zeros_like(resid)
    taps_table = taps_ref[...]
    place = lax.broadcasted_iota(jnp.int32, (UVT, CAP), 0).astype(F32)

    def some(group, carry):
        for side in range(4):
            at = 4 * group + side
            start = pl.multiple_of(tile_ref[at] * UVT, UVT)
            entry = visit_ref[at]
            weight_row = spread_taps(taps_table, entry[2:3], entry[4:5], place).astype(BF16)
            weight_col = spread_taps(taps_table, entry[3:4], entry[5:6], place)
            partial = dot(grid[:, pl.ds(start, UVT)], weight_row)
            model_real = jnp.sum(partial[:UVT] * weight_col, axis=0, keepdims=True)
            model_imag = jnp.sum(partial[UVT:] * weight_col, axis=0, keepdims=True)
            live = entry[6:7] > 0.5
            real = jnp.where(live, entry[0:1] - model_real, 0.0)
            imag = jnp.where(live, entry[1:2] - model_imag, 0.0)
            spread = jnp.concatenate([real * weight_col, imag * weight_col], axis=0).astype(BF16)
            resid[:, pl.ds(start, UVT)] += dot(spread, weight_row, NT)
        return carry

    lax.fori_loop(0, visit_ref.shape[0] // 4, some, 0)
    blocks = [
        (resid[0:128, at * 128 : at * 128 + 128], resid[128:256, at * 128 : at * 128 + 128])
        for at in range(4)
    ]
    turned = []
    for rho, (real, imag) in enumerate(cross_back(blocks)):
        if rho > 0:
            real, imag = turn_back(real, imag, twiddle[rho, 0:1], twiddle[rho, 1:2])
        turned.append(jnp.concatenate([real, imag], axis=1))
    done = dot(both(back, 1), parts(jnp.concatenate(turned, axis=0), 1), NT)
    for rho in range(4):
        row = 4 * (rho // 2) + rho % 2
        move[pl.ds(row, 128, stride=8), :] = done[:128, rho * 128 : rho * 128 + 128]
        move[pl.ds(row + 2, 128, stride=8), :] = done[128:, rho * 128 : rho * 128 + 128]
    out_ref[...] = move[0:1024, :].astype(BF16)


def back_kernel(got_ref, first, twiddle, second, out_ref, send_ref, move, send):
    move[...] = got_ref[...].astype(F32)
    lines = jnp.concatenate([move[pl.ds(slot, 256, stride=4), :] for slot in range(4)], 1).astype(BF16)
    mixed = dot(first[...], twice(lines, 0))
    for row in range(2):
        at = row * 128
        real = mixed[:256, at : at + 128] - mixed[256:, 256 + at : 384 + at]
        imag = mixed[256:, at : at + 128] + mixed[:256, 256 + at : 384 + at]
        turned = jnp.concatenate(
            [real * twiddle[0] - imag * twiddle[1], real * twiddle[1] + imag * twiddle[0]], axis=1
        )
        done = dot(both(second, 1), parts(turned, 1), NT)
        for half in range(2):
            move[pl.ds(2 * half + row, 128, stride=4), :] = done[:, half * 128 : half * 128 + 128]
    for at in range(BLOCKS):
        piece = move[2 * at : 2 * at + 2, :]
        out_ref[:, at * 128 : at * 128 + 128] = piece
        send[2 * OWNER[at] : 2 * OWNER[at] + 2, :] = piece
    send_ref[...] = send[...].astype(BF16)


def gather_window(blocks, phase):
    real, imag = None, None
    for at, value in enumerate(blocks):
        angle = 2.0 * math.pi * (at * phase % 5) / 5.0
        term = value * math.cos(angle) if at * phase % 5 else value
        real = term if real is None else real + term
        if at * phase % 5:
            term = value * -math.sin(angle)
            imag = term if imag is None else imag + term
    return real, imag


def to_frequency(real, imag, phase, window, side, right, left):
    if phase == 0:
        lines = parts(real, 1)
        table = jnp.concatenate([right[0:128, :], right[0:128, :], right[256:384, :]], axis=0)
    else:
        real, imag = turn_forward(real, imag, window[phase, 0:1], window[phase, 1:2])
        lines = parts(jnp.concatenate([real, imag], axis=1), 1)
        table = both(right, 0)
    mixed = dot(lines, table)
    quarters = [
        (mixed[at * 128 : at * 128 + 128, :128], mixed[at * 128 : at * 128 + 128, 128:])
        for at in range(4)
    ]
    turned = []
    for at, (real, imag) in enumerate(cross_forward(quarters)):
        if at > 0:
            real, imag = turn_forward(real, imag, side[at - 1, 0], side[at - 1, 1])
        turned.append(jnp.concatenate([real, imag], axis=0))
    done = dot(both(left, 1), parts(jnp.concatenate(turned, axis=1), 0))
    return done[:128], done[128:]


def transfer_kernel(turn_ref, *refs):
    blocks = [ref[...].astype(F32) for ref in refs[:QUARTERS]]
    window, side, right, left, out_ref = refs[QUARTERS:]
    for phase in range(PHASES):
        real, imag = None, None
        for at, value in enumerate(blocks):
            place = 2 * (phase * QUARTERS + at)
            term = value * turn_ref[place] if phase else value
            real = term if real is None else real + term
            if phase:
                term = value * turn_ref[place + 1]
                imag = -term if imag is None else imag - term
        out_ref[phase, 0], out_ref[phase, 1] = to_frequency(
            real, imag, phase, window, side, right, left
        )


def conv_kernel(
    first, far_left, near_left, own, near_right, far_right, transfer, window, side, right, left,
    back, window_back, sky_ref, resid_ref, base_ref, *out_refs,
):
    blocks = [
        ref[...].astype(F32) for ref in (far_left, near_left, own, near_right, far_right)
    ]
    total = jnp.zeros((GV, 128), F32)
    for phase in range(PHASES):
        real, imag = gather_window(blocks, phase)
        real, imag = to_frequency(real, imag, phase, window, side, right, left)
        trans_real, trans_imag = transfer[phase, 0], transfer[phase, 1]
        blur = jnp.concatenate(
            [real * trans_real - imag * trans_imag, real * trans_imag + imag * trans_real], axis=0
        )
        mixed = dot(both(back, 1), parts(blur, 0))
        quarters = []
        for at in range(4):
            real, imag = mixed[:128, at * 128 : at * 128 + 128], mixed[128:, at * 128 : at * 128 + 128]
            if at > 0:
                real, imag = turn_back(real, imag, side[at - 1, 0], side[at - 1, 1])
            quarters.append((real, imag))
        lines = [jnp.concatenate([real, imag], axis=1) for real, imag in cross_back(quarters)]
        high, low = window_back[phase, 0:256], window_back[phase, 256:512]
        table = jnp.concatenate([high, high, low], axis=0)
        total = total + dot(parts(jnp.concatenate(lines, axis=0), 1), table)
    resid = resid_ref[...].astype(F32)
    base = base_ref[...].astype(F32)
    sky = step(base, resid) if first else sky_ref[...]
    sky = step(sky, resid - total)
    if first:
        out_refs[0][...] = sky
        out_refs[1][...] = (sky - base).astype(BF16)
    else:
        out_refs[0][...] = sky.astype(BF16)


def step(sky, gradient):
    moved = sky + STEP_SIZE * gradient
    return moved - jnp.clip(moved, -THRESHOLD, THRESHOLD)


def last_kernel(got_ref, out_ref, move):
    move[...] = got_ref[...].astype(F32)
    for at in range(BLOCKS):
        out_ref[:, at * 128 : at * 128 + 128] = move[2 * OWNER[at] : 2 * OWNER[at] + 2, :]


def exchange(rows):
    blocks = rows.reshape(BLOCKS, rows.shape[0] // BLOCKS, 128)
    return lax.all_to_all(blocks, JOINT, 0, 0, tiled=True).reshape(rows.shape)


def halo(block, step):
    pairs = [(OWNER[at], OWNER[(at + step) % BLOCKS]) for at in range(BLOCKS)]
    return lax.ppermute(block, JOINT, pairs)


def around_vis(value, step):
    return lax.ppermute(value, "vis", [(at, (at + step) % N_VIS) for at in range(N_VIS)])


def around_y(value, step):
    pairs = []
    for tile in range(N_TILE):
        at = tile // 2 % QUARTERS
        pairs.append((tile, tile + 2 * ((at + step) % QUARTERS - at)))
    return lax.ppermute(value, "tile", pairs)


def shards(
    model_image, psf, kernel_table, observed, visit_tile, visit_count, cell_offset, kernel_row
):
    at_vis = lax.axis_index("vis")
    at_y = lax.axis_index("tile") // 2 % QUARTERS
    tables = TABLES

    live = jnp.arange(CAP)[None, :] < visit_count[0][:, None]
    tile_row = jnp.broadcast_to((visit_tile[0] % 4)[:, None], live.shape)
    packed = jnp.stack(
        [
            observed[0, 0],
            observed[1, 0],
            cell_offset[0, 0].astype(F32),
            cell_offset[1, 0].astype(F32),
            kernel_row[0, 0].astype(F32),
            kernel_row[1, 0].astype(F32),
            live.astype(F32),
            tile_row.astype(F32),
        ],
        axis=1,
    )
    pieces = [lax.dynamic_slice_in_dim(packed, at_vis * 4, 4, 0)]
    for hop in range(1, N_VIS):
        group = lax.dynamic_slice_in_dim(packed, (at_vis + hop) % N_VIS * 4, 4, 0)
        pieces.append(around_vis(group, hop))
    visits = jnp.concatenate(pieces, axis=0)

    send = call(
        row_kernel,
        [shape((8 * BLOCKS, 128), BF16)],
        model_image,
        psf,
        tables["point_right"],
        tables["half_twiddle"],
        tables["row_twiddle"],
        tables["point_left"],
        vmem=60,
        scratch=[pltpu.VMEM((512, 128), F32), pltpu.VMEM((8 * BLOCKS, 128), F32)],
        flops=2 * 3 * 256 * 256 * 1024,
    )[0]
    got = exchange(send)
    visit_rows = visits[:, 7, 0].astype(jnp.int32)
    taps = jnp.pad(kernel_table.astype(BF16).T, ((0, 8), (0, 0)))

    send, base, quarter = call(
        uv_kernel,
        [shape((4 * BLOCKS, 128), BF16), shape((GV, 128), BF16), shape((GV, 128), BF16)],
        visit_rows,
        got,
        visits,
        taps,
        tables["point_right"],
        tables["point_back"],
        tables["lane_twiddle"],
        smem=(0,),
        scratch=[
            pltpu.VMEM((8 * BLOCKS, 128), F32),
            pltpu.VMEM((256, GV), BF16),
            pltpu.VMEM((256, GV), F32),
            pltpu.VMEM((GV, 128), F32),
        ],
        flops=2 * 7 * 256 * 512 * 512,
    )
    got = exchange(send)
    transfer = call(
        transfer_kernel,
        [shape((PHASES, 2, 128, 4 * 128), F32)],
        lax.dynamic_index_in_dim(jnp.asarray(window_turns()), at_y, 0, keepdims=False),
        quarter,
        *[around_y(quarter, QUARTERS - hop) for hop in range(1, QUARTERS)],
        tables["window_twiddle"],
        tables["side_twiddle"],
        tables["point_right"],
        tables["point_left"],
        smem=(0,),
        flops=2 * PHASES * 3 * 2 * 512 * 256 * 256,
    )[0]
    residual_image, send = call(
        back_kernel,
        [shape((2, GU), F32), shape((2 * BLOCKS, 128), BF16)],
        got,
        tables["back_first"],
        tables["back_twiddle"],
        tables["back_second"],
        scratch=[pltpu.VMEM((4 * BLOCKS, 128), F32), pltpu.VMEM((2 * BLOCKS, 128), F32)],
        flops=2 * 3 * 512 * 512 * 256,
    )

    resid = exchange(send)
    wide = base.astype(F32)
    change = (step(wide, resid.astype(F32)) - wide).astype(BF16)
    sky = wide
    for turn in range(2):
        first = turn == 0
        outs = [shape((GV, 128), F32), shape((GV, 128), BF16)] if first else [shape((GV, 128), BF16)]
        got = call(
            functools.partial(conv_kernel, first),
            outs,
            halo(change, 2),
            halo(change, 1),
            change,
            halo(change, -1),
            halo(change, -2),
            transfer,
            tables["window_twiddle"],
            tables["side_twiddle"],
            tables["point_right"],
            tables["point_left"],
            tables["point_back"],
            tables["window_back"],
            base if first else sky,
            resid,
            base,
            flops=2 * PHASES * 3 * 4 * 512 * 256 * 256,
        )
        if first:
            sky, change = got
    got = exchange(got[0])
    model_next = call(
        last_kernel, [shape((2, GU), F32)], got, scratch=[pltpu.VMEM((2 * BLOCKS, 128), F32)]
    )[0]
    return (model_next, residual_image)


def solution(mesh):
    placed = (
        P(("tile", "vis"), None),
        P(("tile", "vis"), None),
        P(),
        P(None, "vis", "tile", None),
        P("vis", "tile"),
        P("vis", "tile"),
        P(None, "vis", "tile", None),
        P(None, "vis", "tile", None),
    )
    return jax.shard_map(
        shards,
        mesh=mesh,
        in_specs=placed,
        out_specs=(P(("tile", "vis"), None), P(("tile", "vis"), None)),
        check_vma=False,
    )
```

```python
import functools
import math

import jax
import jax.numpy as jnp
import numpy as np
from jax import lax
from jax.experimental import pallas as pl
from jax.experimental.pallas import tpu as pltpu
from jax.sharding import PartitionSpec as P

GU = 32768
GV = 512
UVT = 128
CAP = 256
N_TILE = 64
N_VIS = 4
BLOCKS = N_TILE * N_VIS
WIDTH = GU // BLOCKS
HALO = 640
PHASES = 3
QUARTERS = 4
STEP_SIZE = 0.5
THRESHOLD = 0.05
JOINT = ("tile", "vis")
F32 = jnp.float32
BF16 = jnp.bfloat16
NN = (((1,), (0,)), ((), ()))
NT = (((1,), (1,)), ((), ()))
TN = (((0,), (0,)), ((), ()))
MIB = 1024 * 1024


def angles(left, right, length):
    return 2.0 * math.pi / length * ((np.asarray(left)[:, None] * np.asarray(right)[None, :]) % length)


def split_table(table, axis):
    table = np.asarray(table, np.float32)
    high = table.astype(jnp.bfloat16)
    low = (table - high.astype(np.float32)).astype(jnp.bfloat16)
    return np.concatenate([high, low], axis)


def block_owner():
    owner = []
    for run in range(16):
        x, y = run // 4, run % 4
        y = y if x % 2 == 0 else 3 - y
        for spot in range(8):
            z = spot if run % 2 == 0 else 7 - spot
            for core in range(2):
                owner.append((((x * 2 + z // 4) * 4 + y) * 2 + core) * 4 + z % 4)
    return owner


def build_tables():
    tables = {}
    scale = 1.0 / math.sqrt(GV * GU)
    first = angles(np.arange(256), np.arange(256), 256)
    second = angles(np.arange(128), np.arange(128), 128)
    cosine, sine = np.cos(second), np.sin(second)
    twiddle = angles(np.arange(128), np.arange(256), GU)
    tables["row_twiddle"] = (np.stack([np.cos(twiddle), -np.sin(twiddle)]) * scale).astype(np.float32)
    half = angles([1], np.arange(128), 256)
    tables["half_twiddle"] = np.concatenate([np.cos(half), np.sin(half)]).astype(np.float32)
    tables["back_first"] = split_table(np.concatenate([np.cos(first), np.sin(first)], 0), 1)
    tables["back_twiddle"] = np.stack([np.cos(twiddle.T), np.sin(twiddle.T)]).astype(np.float32)
    tables["back_second"] = split_table(np.concatenate([cosine, -sine], 1) * scale, 1)
    block = np.block([[cosine, -sine], [sine, cosine]])
    tables["point_right"] = split_table(block, 0)
    tables["point_left"] = split_table(block.T, 1)
    tables["point_back"] = split_table(block, 1)
    quarter = angles(np.arange(4), np.arange(128), GV)
    tables["lane_twiddle"] = np.stack([np.cos(quarter), np.sin(quarter)], 1).astype(np.float32)
    rows = np.stack([np.cos(quarter[1:]), np.sin(quarter[1:])], 1)[:, :, :, None]
    tables["side_twiddle"] = np.broadcast_to(rows, (3, 2, 128, 128)).astype(np.float32)
    right, back = [], []
    for phase in range(PHASES):
        turn = angles(np.arange(128), 5 * np.arange(128) + phase, HALO)
        turn = np.block([[np.cos(turn), -np.sin(turn)], [np.sin(turn), np.cos(turn)]])
        right.append(split_table(turn, 0))
        share = (1.0 if phase == 0 else 2.0) / (GV * HALO)
        turn = angles(5 * np.arange(128) + phase, 256 + np.arange(128), HALO)
        back.append(split_table(np.concatenate([np.cos(turn), -np.sin(turn)], 0) * share, 0))
    tables["window_right"] = np.stack(right)
    tables["window_back"] = np.stack(back)
    return tables


TABLES = build_tables()
OWNER = block_owner()


def window_turns():
    place = np.array([3, 4, 0, 1])
    out = np.zeros((QUARTERS, PHASES, QUARTERS, 2), np.float32)
    for at in range(QUARTERS):
        for phase in range(PHASES):
            for block in range(QUARTERS):
                turn = 2.0 * math.pi * (place[(at + block) % QUARTERS] * phase % 5) / 5.0
                out[at, phase, block] = (math.cos(turn), math.sin(turn))
    return out.reshape(QUARTERS, -1)


def dot(left, right, dims=NN):
    return lax.dot_general(left, right, dims, preferred_element_type=F32)


def parts(value, axis):
    high = value.astype(BF16)
    low = (value - high.astype(F32)).astype(BF16)
    return jnp.concatenate([high, low, high], axis=axis)


def both(table, axis):
    high, low = jnp.split(table[...], 2, axis=axis)
    return jnp.concatenate([high, high, low], axis=axis)


def twice(value, axis):
    return jnp.concatenate([value, value], axis=axis)


def call(kernel, outs, *args, smem=(), scratch=(), flops=0, vmem=32):
    specs = [
        pl.BlockSpec(memory_space=pltpu.SMEM if at in smem else pltpu.VMEM) for at in range(len(args))
    ]
    size = sum(int(np.prod(a.shape)) * a.dtype.itemsize for a in args)
    size += sum(int(np.prod(o.shape)) * o.dtype.itemsize for o in outs)
    return pl.pallas_call(
        kernel,
        out_shape=outs,
        in_specs=specs,
        out_specs=[pl.BlockSpec(memory_space=pltpu.VMEM)] * len(outs),
        scratch_shapes=list(scratch),
        compiler_params=pltpu.CompilerParams(vmem_limit_bytes=vmem * MIB),
        cost_estimate=pl.CostEstimate(flops=flops, bytes_accessed=size, transcendentals=0),
    )(*args)


def shape(dims, dtype):
    return jax.ShapeDtypeStruct(dims, dtype)


def cross_forward(blocks):
    (r0, i0), (r1, i1), (r2, i2), (r3, i3) = blocks
    ar, ai, br, bi = r0 + r2, i0 + i2, r0 - r2, i0 - i2
    cr, ci, dr, di = r1 + r3, i1 + i3, r1 - r3, i1 - i3
    return [(ar + cr, ai + ci), (br + di, bi - dr), (ar - cr, ai - ci), (br - di, bi + dr)]


def cross_back(blocks):
    (r0, i0), (r1, i1), (r2, i2), (r3, i3) = blocks
    ar, ai, br, bi = r0 + r2, i0 + i2, r0 - r2, i0 - i2
    cr, ci, dr, di = r1 + r3, i1 + i3, r1 - r3, i1 - i3
    return [(ar + cr, ai + ci), (br - di, bi + dr), (ar - cr, ai - ci), (br + di, bi - dr)]


def turn_forward(real, imag, cosine, sine):
    return real * cosine + imag * sine, imag * cosine - real * sine


def turn_back(real, imag, cosine, sine):
    return real * cosine - imag * sine, imag * cosine + real * sine


def row_kernel(sky_ref, psf_ref, right, half_turn, twiddle, left, out_ref, lines, send):
    for at in range(BLOCKS):
        piece = sky_ref[:, at * 128 : at * 128 + 128]
        lines[2 * at : 2 * at + 2, :] = piece
        row = 8 * OWNER[at] + 4
        send[row : row + 2, :] = piece
    for at in range(QUARTERS):
        piece = psf_ref[:, at * 128 : at * 128 + 128]
        for device in range(BLOCKS):
            if device // 8 % QUARTERS == at:
                send[8 * device + 6 : 8 * device + 8, :] = piece
    pieces = [
        lines[pl.ds(2 * odd + row, 128, stride=4), :] for row in range(2) for odd in range(2)
    ]
    high, low = right[0:128, :], right[256:384, :]
    mixed = dot(parts(jnp.concatenate(pieces, 1), 0), jnp.concatenate([high, high, low], 0), TN)
    for row in range(2):
        even = mixed[row * 256 : row * 256 + 128]
        odd = mixed[row * 256 + 128 : row * 256 + 256]
        odd_real, odd_imag = turn_forward(odd[:, :128], odd[:, 128:], half_turn[0:1], half_turn[1:2])
        real = jnp.concatenate([even[:, :128] + odd_real, even[:, :128] - odd_real], axis=1)
        imag = jnp.concatenate([even[:, 128:] + odd_imag, even[:, 128:] - odd_imag], axis=1)
        turned = jnp.concatenate(
            [real * twiddle[0] - imag * twiddle[1], real * twiddle[1] + imag * twiddle[0]], axis=0
        )
        done = dot(both(left, 1), parts(turned, 0))
        for half in range(2):
            send[pl.ds(8 * half + row, 128, stride=16), :] = done[:128, half * 128 : half * 128 + 128]
            send[pl.ds(8 * half + 2 + row, 128, stride=16), :] = done[128:, half * 128 : half * 128 + 128]
    out_ref[...] = send[...].astype(BF16)


def spread_taps(taps_table, offset, row, place):
    index = jnp.broadcast_to(row.astype(jnp.int32), (8, CAP))
    taps = jnp.concatenate(
        [
            jnp.take_along_axis(taps_table, index[:, at : at + 128], axis=1, mode="promise_in_bounds")
            for at in range(0, CAP, 128)
        ],
        axis=1,
    )
    turn = (place[0:8].astype(jnp.int32) - offset.astype(jnp.int32)) & 7
    turned = jnp.zeros((8, CAP), F32)
    for shift in range(8):
        turned = jnp.where(turn == shift, taps[shift : shift + 1, :], turned)
    within = place - offset
    keep = jnp.abs(within - 3.5) < 4.0
    return jnp.where(keep, jnp.concatenate([turned] * (UVT // 8), axis=0), 0.0)


def uv_kernel(
    tile_ref, got_ref, group_0, group_1, group_2, group_3, taps_ref, right, back, twiddle,
    out_ref, base_ref, psf_ref, move, grid, resid, side, visits,
):
    for at, group in enumerate((group_0, group_1, group_2, group_3)):
        visits[32 * at : 32 * at + 32, :] = group[...].astype(F32)[0:32]
    move[...] = got_ref[...].astype(F32)
    for slot, ref in ((4, base_ref), (6, psf_ref)):
        for row in range(2):
            side[pl.ds(row, 256, stride=2), :] = move[pl.ds(slot + row, 256, stride=8), :]
        ref[...] = side[...].astype(BF16)
    lines = []
    for rho in range(4):
        row = 8 * (rho // 2) + rho % 2
        lines.append(
            jnp.concatenate(
                [move[pl.ds(row, 128, stride=16), :], move[pl.ds(row + 2, 128, stride=16), :]], 0
            )
        )
    lines = jnp.concatenate(lines, axis=1).astype(BF16)
    mixed = dot(twice(lines, 0), right[...], TN)
    blocks = []
    for rho in range(4):
        real, imag = mixed[rho * 128 : rho * 128 + 128, :128], mixed[rho * 128 : rho * 128 + 128, 128:]
        if rho > 0:
            real, imag = turn_forward(real, imag, twiddle[rho, 0:1], twiddle[rho, 1:2])
        blocks.append((real, imag))
    for at, (real, imag) in enumerate(cross_forward(blocks)):
        grid[0:128, at * 128 : at * 128 + 128] = real.astype(BF16)
        grid[128:256, at * 128 : at * 128 + 128] = imag.astype(BF16)
    resid[...] = jnp.zeros_like(resid)
    taps_table = taps_ref[...].astype(F32)[0:8]
    place = lax.broadcasted_iota(jnp.int32, (UVT, CAP), 0).astype(F32)

    def some(group, carry):
        for side in range(4):
            at = 4 * group + side
            start = pl.multiple_of(tile_ref[at] * UVT, UVT)
            entry = visits[pl.ds(pl.multiple_of(8 * at, 8), 8), :]
            weight_row = spread_taps(taps_table, entry[4:5], entry[6:7], place).astype(BF16)
            weight_col = spread_taps(taps_table, entry[5:6], entry[7:8], place)
            partial = dot(grid[:, pl.ds(start, UVT)], weight_row)
            model_real = jnp.sum(partial[:UVT] * weight_col, axis=0, keepdims=True)
            model_imag = jnp.sum(partial[UVT:] * weight_col, axis=0, keepdims=True)
            real = entry[0:1] + entry[1:2] - model_real
            imag = entry[2:3] + entry[3:4] - model_imag
            spread = jnp.concatenate([real * weight_col, imag * weight_col], axis=0).astype(BF16)
            resid[:, pl.ds(start, UVT)] += dot(spread, weight_row, NT)
        return carry

    lax.fori_loop(0, 4, some, 0)
    blocks = [
        (resid[0:128, at * 128 : at * 128 + 128], resid[128:256, at * 128 : at * 128 + 128])
        for at in range(4)
    ]
    turned = []
    for rho, (real, imag) in enumerate(cross_back(blocks)):
        if rho > 0:
            real, imag = turn_back(real, imag, twiddle[rho, 0:1], twiddle[rho, 1:2])
        turned.append(jnp.concatenate([real, imag], axis=1))
    done = dot(both(back, 1), parts(jnp.concatenate(turned, axis=0), 1), NT)
    for rho in range(4):
        row = 4 * (rho // 2) + rho % 2
        move[pl.ds(row, 128, stride=8), :] = done[:128, rho * 128 : rho * 128 + 128]
        move[pl.ds(row + 2, 128, stride=8), :] = done[128:, rho * 128 : rho * 128 + 128]
    out_ref[...] = move[0:1024, :].astype(BF16)


def back_kernel(got_ref, first, twiddle, second, out_ref, send_ref, move, send):
    move[...] = got_ref[...].astype(F32)
    lines = jnp.concatenate([move[pl.ds(slot, 256, stride=4), :] for slot in range(4)], 1).astype(BF16)
    mixed = dot(first[...], twice(lines, 0))
    for row in range(2):
        at = row * 128
        real = mixed[:256, at : at + 128] - mixed[256:, 256 + at : 384 + at]
        imag = mixed[256:, at : at + 128] + mixed[:256, 256 + at : 384 + at]
        turned = jnp.concatenate(
            [real * twiddle[0] - imag * twiddle[1], real * twiddle[1] + imag * twiddle[0]], axis=1
        )
        done = dot(both(second, 1), parts(turned, 1), NT)
        for half in range(2):
            move[pl.ds(2 * half + row, 128, stride=4), :] = done[:, half * 128 : half * 128 + 128]
    for at in range(BLOCKS):
        piece = move[2 * at : 2 * at + 2, :]
        out_ref[:, at * 128 : at * 128 + 128] = piece
        send[2 * OWNER[at] : 2 * OWNER[at] + 2, :] = piece
    send_ref[...] = send[...].astype(BF16)


def gather_window(blocks):
    c1, c2 = math.cos(0.4 * math.pi), math.cos(0.8 * math.pi)
    s1, s2 = math.sin(0.4 * math.pi), math.sin(0.8 * math.pi)
    x0, x1, x2, x3, x4 = blocks
    p1, m1, p2, m2 = x1 + x4, x1 - x4, x2 + x3, x2 - x3
    return [
        (x0 + p1 + p2, None),
        (x0 + c1 * p1 + c2 * p2, -s1 * m1 - s2 * m2),
        (x0 + c2 * p1 + c1 * p2, s1 * m2 - s2 * m1),
    ]


def to_frequency(real, imag, right, side, left):
    if imag is None:
        lines = parts(real, 1)
        table = jnp.concatenate([right[0:128, :], right[0:128, :], right[256:384, :]], axis=0)
    else:
        lines = parts(jnp.concatenate([real, imag], axis=1), 1)
        table = both(right, 0)
    mixed = dot(lines, table)
    quarters = [
        (mixed[at * 128 : at * 128 + 128, :128], mixed[at * 128 : at * 128 + 128, 128:])
        for at in range(4)
    ]
    turned = []
    for at, (real, imag) in enumerate(cross_forward(quarters)):
        if at > 0:
            real, imag = turn_forward(real, imag, side[at - 1, 0], side[at - 1, 1])
        turned.append(jnp.concatenate([real, imag], axis=0))
    done = dot(both(left, 1), parts(jnp.concatenate(turned, axis=1), 0))
    return done[:128], done[128:]


def transfer_kernel(turn_ref, *refs):
    blocks = [ref[...].astype(F32) for ref in refs[:QUARTERS]]
    side, right, left, out_ref = refs[QUARTERS:]
    for phase in range(PHASES):
        real, imag = None, None
        for at, value in enumerate(blocks):
            place = 2 * (phase * QUARTERS + at)
            term = value * turn_ref[place] if phase else value
            real = term if real is None else real + term
            if phase:
                term = value * turn_ref[place + 1]
                imag = -term if imag is None else imag - term
        out_ref[phase, 0], out_ref[phase, 1] = to_frequency(
            real, imag, right.at[phase], side, left
        )


def conv_kernel(
    first, far_left, near_left, own, near_right, far_right, transfer, side, right, left,
    back, window_back, sky_ref, resid_ref, base_ref, *out_refs,
):
    blocks = [
        ref[...].astype(F32) for ref in (far_left, near_left, own, near_right, far_right)
    ]
    windows = gather_window(blocks)
    total = jnp.zeros((GV, 128), F32)
    for phase in range(PHASES):
        real, imag = to_frequency(*windows[phase], right.at[phase], side, left)
        trans_real, trans_imag = transfer[phase, 0], transfer[phase, 1]
        blur = jnp.concatenate(
            [real * trans_real - imag * trans_imag, real * trans_imag + imag * trans_real], axis=0
        )
        mixed = dot(both(back, 1), parts(blur, 0))
        quarters = []
        for at in range(4):
            real, imag = mixed[:128, at * 128 : at * 128 + 128], mixed[128:, at * 128 : at * 128 + 128]
            if at > 0:
                real, imag = turn_back(real, imag, side[at - 1, 0], side[at - 1, 1])
            quarters.append((real, imag))
        lines = [jnp.concatenate([real, imag], axis=1) for real, imag in cross_back(quarters)]
        high, low = window_back[phase, 0:256], window_back[phase, 256:512]
        table = jnp.concatenate([high, high, low], axis=0)
        total = total + dot(parts(jnp.concatenate(lines, axis=0), 1), table)
    resid = resid_ref[...].astype(F32)
    base = base_ref[...].astype(F32)
    sky = step(base, resid) if first else sky_ref[...]
    sky = step(sky, resid - total)
    if first:
        out_refs[0][...] = sky
        out_refs[1][...] = (sky - base).astype(BF16)
    else:
        out_refs[0][...] = sky.astype(BF16)


def step(sky, gradient):
    moved = sky + STEP_SIZE * gradient
    return moved - jnp.clip(moved, -THRESHOLD, THRESHOLD)


def last_kernel(got_ref, out_ref, move):
    move[...] = got_ref[...].astype(F32)
    for at in range(BLOCKS):
        out_ref[:, at * 128 : at * 128 + 128] = move[2 * OWNER[at] : 2 * OWNER[at] + 2, :]


def exchange(rows):
    blocks = rows.reshape(BLOCKS, rows.shape[0] // BLOCKS, 128)
    return lax.all_to_all(blocks, JOINT, 0, 0, tiled=True).reshape(rows.shape)


def halo(block, step):
    pairs = [(OWNER[at], OWNER[(at + step) % BLOCKS]) for at in range(BLOCKS)]
    return lax.ppermute(block, JOINT, pairs)


def around_vis(value, step):
    return lax.ppermute(value, "vis", [(at, (at + step) % N_VIS) for at in range(N_VIS)])


def around_y(value, step):
    pairs = []
    for tile in range(N_TILE):
        at = tile // 2 % QUARTERS
        pairs.append((tile, tile + 2 * ((at + step) % QUARTERS - at)))
    return lax.ppermute(value, "tile", pairs)


def shards(
    model_image, psf, kernel_table, observed, visit_tile, visit_count, cell_offset, kernel_row
):
    at_vis = lax.axis_index("vis")
    at_y = lax.axis_index("tile") // 2 % QUARTERS
    tables = TABLES

    live = jnp.arange(CAP)[None, :] < visit_count[0][:, None]
    wide = observed[:, 0] * 65537.0
    high = wide - (wide - observed[:, 0])
    low = observed[:, 0] - high
    rows = [high[0], low[0], high[1], low[1], jnp.where(live, cell_offset[0, 0], 2 * UVT)]
    rows += [cell_offset[1, 0], kernel_row[0, 0], kernel_row[1, 0]]
    packed = jnp.stack([row.astype(BF16) for row in rows], axis=1).reshape(4, 32, CAP)
    tile_row = (visit_tile[0] % 4).astype(BF16).reshape(4, 4, 1)
    tile_row = jnp.pad(jnp.broadcast_to(tile_row, (4, 4, CAP)), ((0, 0), (0, 4), (0, 0)))
    packed = jnp.concatenate([packed, tile_row], axis=1)
    groups = [lax.dynamic_index_in_dim(packed, at_vis, 0, keepdims=False)]
    for hop in range(1, N_VIS):
        group = lax.dynamic_index_in_dim(packed, (at_vis + hop) % N_VIS, 0, keepdims=False)
        groups.append(around_vis(group, hop))

    send = call(
        row_kernel,
        [shape((8 * BLOCKS, 128), BF16)],
        model_image,
        psf,
        tables["point_right"],
        tables["half_twiddle"],
        tables["row_twiddle"],
        tables["point_left"],
        vmem=60,
        scratch=[pltpu.VMEM((512, 128), F32), pltpu.VMEM((8 * BLOCKS, 128), F32)],
        flops=2 * 3 * 256 * 256 * 1024,
    )[0]
    got = exchange(send)
    visit_rows = jnp.concatenate([group[32:36, 0] for group in groups]).astype(jnp.int32)
    taps = jnp.pad(kernel_table.astype(BF16).T, ((0, 8), (0, 0)))

    send, base, quarter = call(
        uv_kernel,
        [shape((4 * BLOCKS, 128), BF16), shape((GV, 128), BF16), shape((GV, 128), BF16)],
        visit_rows,
        got,
        *groups,
        taps,
        tables["point_right"],
        tables["point_back"],
        tables["lane_twiddle"],
        smem=(0,),
        scratch=[
            pltpu.VMEM((8 * BLOCKS, 128), F32),
            pltpu.VMEM((256, GV), BF16),
            pltpu.VMEM((256, GV), F32),
            pltpu.VMEM((GV, 128), F32),
            pltpu.VMEM((128, CAP), F32),
        ],
        flops=2 * 7 * 256 * 512 * 512,
    )
    got = exchange(send)
    transfer = call(
        transfer_kernel,
        [shape((PHASES, 2, 128, 4 * 128), F32)],
        lax.dynamic_index_in_dim(jnp.asarray(window_turns()), at_y, 0, keepdims=False),
        quarter,
        *[around_y(quarter, QUARTERS - hop) for hop in range(1, QUARTERS)],
        tables["side_twiddle"],
        tables["window_right"],
        tables["point_left"],
        smem=(0,),
        flops=2 * PHASES * 3 * 2 * 512 * 256 * 256,
    )[0]
    residual_image, send = call(
        back_kernel,
        [shape((2, GU), F32), shape((2 * BLOCKS, 128), BF16)],
        got,
        tables["back_first"],
        tables["back_twiddle"],
        tables["back_second"],
        scratch=[pltpu.VMEM((4 * BLOCKS, 128), F32), pltpu.VMEM((2 * BLOCKS, 128), F32)],
        flops=2 * 3 * 512 * 512 * 256,
    )

    resid = exchange(send)
    wide = base.astype(F32)
    change = (step(wide, resid.astype(F32)) - wide).astype(BF16)
    sky = wide
    for turn in range(2):
        first = turn == 0
        outs = [shape((GV, 128), F32), shape((GV, 128), BF16)] if first else [shape((GV, 128), BF16)]
        got = call(
            functools.partial(conv_kernel, first),
            outs,
            halo(change, 2),
            halo(change, 1),
            change,
            halo(change, -1),
            halo(change, -2),
            transfer,
            tables["side_twiddle"],
            tables["window_right"],
            tables["point_left"],
            tables["point_back"],
            tables["window_back"],
            base if first else sky,
            resid,
            base,
            flops=2 * PHASES * 3 * 4 * 512 * 256 * 256,
        )
        if first:
            sky, change = got
    got = exchange(got[0])
    model_next = call(
        last_kernel, [shape((2, GU), F32)], got, scratch=[pltpu.VMEM((2 * BLOCKS, 128), F32)]
    )[0]
    return (model_next, residual_image)


def solution(mesh):
    placed = (
        P(("tile", "vis"), None),
        P(("tile", "vis"), None),
        P(),
        P(None, "vis", "tile", None),
        P("vis", "tile"),
        P("vis", "tile"),
        P(None, "vis", "tile", None),
        P(None, "vis", "tile", None),
    )
    return jax.shard_map(
        shards,
        mesh=mesh,
        in_specs=placed,
        out_specs=(P(("tile", "vis"), None), P(("tile", "vis"), None)),
        check_vma=False,
    )
```

```python
import functools
import math

import jax
import jax.numpy as jnp
import numpy as np
from jax import lax
from jax.experimental import pallas as pl
from jax.experimental.pallas import tpu as pltpu
from jax.sharding import PartitionSpec as P

GU = 32768
GV = 512
UVT = 128
CAP = 256
N_TILE = 64
N_VIS = 4
BLOCKS = N_TILE * N_VIS
WIDTH = GU // BLOCKS
HALO = 640
PHASES = 3
QUARTERS = 4
STEP_SIZE = 0.5
THRESHOLD = 0.05
JOINT = ("tile", "vis")
F32 = jnp.float32
BF16 = jnp.bfloat16
NN = (((1,), (0,)), ((), ()))
NT = (((1,), (1,)), ((), ()))
TN = (((0,), (0,)), ((), ()))
MIB = 1024 * 1024


def angles(left, right, length):
    return 2.0 * math.pi / length * ((np.asarray(left)[:, None] * np.asarray(right)[None, :]) % length)


def split_table(table, axis):
    table = np.asarray(table, np.float32)
    high = table.astype(jnp.bfloat16)
    low = (table - high.astype(np.float32)).astype(jnp.bfloat16)
    return np.concatenate([high, low], axis)


def block_owner():
    owner = []
    for run in range(16):
        x, y = run // 4, run % 4
        y = y if x % 2 == 0 else 3 - y
        for spot in range(8):
            z = spot if run % 2 == 0 else 7 - spot
            for core in range(2):
                owner.append((((x * 2 + z // 4) * 4 + y) * 2 + core) * 4 + z % 4)
    return owner


def build_tables():
    tables = {}
    scale = 1.0 / math.sqrt(GV * GU)
    first = angles(np.arange(256), np.arange(256), 256)
    second = angles(np.arange(128), np.arange(128), 128)
    cosine, sine = np.cos(second), np.sin(second)
    twiddle = angles(np.arange(128), np.arange(256), GU)
    tables["row_twiddle"] = (np.stack([np.cos(twiddle), -np.sin(twiddle)]) * scale).astype(np.float32)
    half = angles([1], np.arange(128), 256)
    tables["half_twiddle"] = np.concatenate([np.cos(half), np.sin(half)]).astype(np.float32)
    tables["back_first"] = split_table(np.concatenate([np.cos(first), np.sin(first)], 0), 1)
    tables["back_twiddle"] = np.stack([np.cos(twiddle.T), np.sin(twiddle.T)]).astype(np.float32)
    tables["back_second"] = split_table(np.concatenate([cosine, -sine], 1) * scale, 1)
    block = np.block([[cosine, -sine], [sine, cosine]])
    tables["point_right"] = split_table(block, 0)
    tables["point_left"] = split_table(block.T, 1)
    tables["point_back"] = split_table(block, 1)
    quarter = angles(np.arange(4), np.arange(128), GV)
    tables["lane_twiddle"] = np.stack([np.cos(quarter), np.sin(quarter)], 1).astype(np.float32)
    rows = np.stack([np.cos(quarter[1:]), np.sin(quarter[1:])], 1)[:, :, :, None]
    tables["side_twiddle"] = np.broadcast_to(rows, (3, 2, 128, 128)).astype(np.float32)
    right, back = [], []
    for phase in range(PHASES):
        turn = angles(np.arange(128), 5 * np.arange(128) + phase, HALO)
        turn = np.block([[np.cos(turn), -np.sin(turn)], [np.sin(turn), np.cos(turn)]])
        right.append(split_table(turn, 0))
        share = (1.0 if phase == 0 else 2.0) / (GV * HALO)
        turn = angles(5 * np.arange(128) + phase, np.arange(128), HALO)
        back.append(split_table(np.concatenate([np.cos(turn), -np.sin(turn)], 0) * share, 0))
    tables["window_right"] = np.stack(right)
    tables["window_back"] = np.stack(back)
    return tables


TABLES = build_tables()
OWNER = block_owner()


def window_turns():
    place = np.array([3, 4, 0, 1])
    out = np.zeros((QUARTERS, PHASES, QUARTERS, 2), np.float32)
    for at in range(QUARTERS):
        for phase in range(PHASES):
            for block in range(QUARTERS):
                turn = 2.0 * math.pi * (place[(at + block) % QUARTERS] * phase % 5) / 5.0
                out[at, phase, block] = (math.cos(turn), math.sin(turn))
    return out.reshape(QUARTERS, -1)


def dot(left, right, dims=NN):
    return lax.dot_general(left, right, dims, preferred_element_type=F32)


def parts(value, axis):
    high = value.astype(BF16)
    low = (value - high.astype(F32)).astype(BF16)
    return jnp.concatenate([high, low, high], axis=axis)


def both(table, axis):
    high, low = jnp.split(table[...], 2, axis=axis)
    return jnp.concatenate([high, high, low], axis=axis)


def twice(value, axis):
    return jnp.concatenate([value, value], axis=axis)


def call(kernel, outs, *args, smem=(), scratch=(), flops=0, vmem=32):
    specs = [
        pl.BlockSpec(memory_space=pltpu.SMEM if at in smem else pltpu.VMEM) for at in range(len(args))
    ]
    size = sum(int(np.prod(a.shape)) * a.dtype.itemsize for a in args)
    size += sum(int(np.prod(o.shape)) * o.dtype.itemsize for o in outs)
    return pl.pallas_call(
        kernel,
        out_shape=outs,
        in_specs=specs,
        out_specs=[pl.BlockSpec(memory_space=pltpu.VMEM)] * len(outs),
        scratch_shapes=list(scratch),
        compiler_params=pltpu.CompilerParams(vmem_limit_bytes=vmem * MIB),
        cost_estimate=pl.CostEstimate(flops=flops, bytes_accessed=size, transcendentals=0),
    )(*args)


def shape(dims, dtype):
    return jax.ShapeDtypeStruct(dims, dtype)


def cross_forward(blocks):
    (r0, i0), (r1, i1), (r2, i2), (r3, i3) = blocks
    ar, ai, br, bi = r0 + r2, i0 + i2, r0 - r2, i0 - i2
    cr, ci, dr, di = r1 + r3, i1 + i3, r1 - r3, i1 - i3
    return [(ar + cr, ai + ci), (br + di, bi - dr), (ar - cr, ai - ci), (br - di, bi + dr)]


def cross_back(blocks):
    (r0, i0), (r1, i1), (r2, i2), (r3, i3) = blocks
    ar, ai, br, bi = r0 + r2, i0 + i2, r0 - r2, i0 - i2
    cr, ci, dr, di = r1 + r3, i1 + i3, r1 - r3, i1 - i3
    return [(ar + cr, ai + ci), (br - di, bi + dr), (ar - cr, ai - ci), (br + di, bi - dr)]


def turn_forward(real, imag, cosine, sine):
    return real * cosine + imag * sine, imag * cosine - real * sine


def turn_back(real, imag, cosine, sine):
    return real * cosine - imag * sine, imag * cosine + real * sine


def row_kernel(sky_ref, psf_ref, right, half_turn, twiddle, left, out_ref, lines, send):
    for at in range(BLOCKS):
        piece = sky_ref[:, at * 128 : at * 128 + 128]
        lines[2 * at : 2 * at + 2, :] = piece
        row = 8 * OWNER[at] + 4
        send[row : row + 2, :] = piece
    for at in range(QUARTERS):
        piece = psf_ref[:, at * 128 : at * 128 + 128]
        for device in range(BLOCKS):
            if device // 8 % QUARTERS == at:
                send[8 * device + 6 : 8 * device + 8, :] = piece
    pieces = [
        lines[pl.ds(2 * odd + row, 128, stride=4), :] for row in range(2) for odd in range(2)
    ]
    high, low = right[0:128, :], right[256:384, :]
    mixed = dot(parts(jnp.concatenate(pieces, 1), 0), jnp.concatenate([high, high, low], 0), TN)
    for row in range(2):
        even = mixed[row * 256 : row * 256 + 128]
        odd = mixed[row * 256 + 128 : row * 256 + 256]
        odd_real, odd_imag = turn_forward(odd[:, :128], odd[:, 128:], half_turn[0:1], half_turn[1:2])
        real = jnp.concatenate([even[:, :128] + odd_real, even[:, :128] - odd_real], axis=1)
        imag = jnp.concatenate([even[:, 128:] + odd_imag, even[:, 128:] - odd_imag], axis=1)
        turned = jnp.concatenate(
            [real * twiddle[0] - imag * twiddle[1], real * twiddle[1] + imag * twiddle[0]], axis=0
        )
        done = dot(both(left, 1), parts(turned, 0))
        for half in range(2):
            send[pl.ds(8 * half + row, 128, stride=16), :] = done[:128, half * 128 : half * 128 + 128]
            send[pl.ds(8 * half + 2 + row, 128, stride=16), :] = done[128:, half * 128 : half * 128 + 128]
    out_ref[...] = send[...].astype(BF16)


def spread_taps(taps_table, offset, row, place):
    index = jnp.broadcast_to(row.astype(jnp.int32), (8, CAP))
    taps = jnp.concatenate(
        [
            jnp.take_along_axis(taps_table, index[:, at : at + 128], axis=1, mode="promise_in_bounds")
            for at in range(0, CAP, 128)
        ],
        axis=1,
    )
    turn = (place[0:8].astype(jnp.int32) - offset.astype(jnp.int32)) & 7
    turned = jnp.zeros((8, CAP), F32)
    for shift in range(8):
        turned = jnp.where(turn == shift, taps[shift : shift + 1, :], turned)
    within = place - offset
    keep = jnp.abs(within - 3.5) < 4.0
    return jnp.where(keep, jnp.concatenate([turned] * (UVT // 8), axis=0), 0.0)


def uv_kernel(
    tile_ref, got_ref, group_0, group_1, group_2, group_3, taps_ref, right, back, twiddle,
    out_ref, base_ref, psf_ref, move, grid, resid, side, visits,
):
    for at, group in enumerate((group_0, group_1, group_2, group_3)):
        visits[32 * at : 32 * at + 32, :] = group[...].astype(F32)[0:32]
    move[...] = got_ref[...].astype(F32)
    for slot, ref in ((4, base_ref), (6, psf_ref)):
        for row in range(2):
            side[pl.ds(row, 256, stride=2), :] = move[pl.ds(slot + row, 256, stride=8), :]
        ref[...] = side[...].astype(BF16)
    lines = []
    for rho in range(4):
        row = 8 * (rho // 2) + rho % 2
        lines.append(
            jnp.concatenate(
                [move[pl.ds(row, 128, stride=16), :], move[pl.ds(row + 2, 128, stride=16), :]], 0
            )
        )
    lines = jnp.concatenate(lines, axis=1).astype(BF16)
    mixed = dot(twice(lines, 0), right[...], TN)
    blocks = []
    for rho in range(4):
        real, imag = mixed[rho * 128 : rho * 128 + 128, :128], mixed[rho * 128 : rho * 128 + 128, 128:]
        if rho > 0:
            real, imag = turn_forward(real, imag, twiddle[rho, 0:1], twiddle[rho, 1:2])
        blocks.append((real, imag))
    for at, (real, imag) in enumerate(cross_forward(blocks)):
        grid[0:128, at * 128 : at * 128 + 128] = real.astype(BF16)
        grid[128:256, at * 128 : at * 128 + 128] = imag.astype(BF16)
    resid[...] = jnp.zeros_like(resid)
    taps_table = taps_ref[...].astype(F32)[0:8]
    place = lax.broadcasted_iota(jnp.int32, (UVT, CAP), 0).astype(F32)

    def some(group, carry):
        for side in range(8):
            at = 8 * group + side
            start = pl.multiple_of(tile_ref[at] * UVT, UVT)
            entry = visits[pl.ds(pl.multiple_of(8 * at, 8), 8), :]
            weight_row = spread_taps(taps_table, entry[4:5], entry[6:7], place).astype(BF16)
            weight_col = spread_taps(taps_table, entry[5:6], entry[7:8], place)
            partial = dot(grid[:, pl.ds(start, UVT)], weight_row)
            model_real = jnp.sum(partial[:UVT] * weight_col, axis=0, keepdims=True)
            model_imag = jnp.sum(partial[UVT:] * weight_col, axis=0, keepdims=True)
            real = entry[0:1] + entry[1:2] - model_real
            imag = entry[2:3] + entry[3:4] - model_imag
            spread = jnp.concatenate([real * weight_col, imag * weight_col], axis=0).astype(BF16)
            resid[:, pl.ds(start, UVT)] += dot(spread, weight_row, NT)
        return carry

    lax.fori_loop(0, 2, some, 0)
    blocks = [
        (resid[0:128, at * 128 : at * 128 + 128], resid[128:256, at * 128 : at * 128 + 128])
        for at in range(4)
    ]
    turned = []
    for rho, (real, imag) in enumerate(cross_back(blocks)):
        if rho > 0:
            real, imag = turn_back(real, imag, twiddle[rho, 0:1], twiddle[rho, 1:2])
        turned.append(jnp.concatenate([real, imag], axis=1))
    done = dot(both(back, 1), parts(jnp.concatenate(turned, axis=0), 1), NT)
    for rho in range(4):
        row = 4 * (rho // 2) + rho % 2
        move[pl.ds(row, 128, stride=8), :] = done[:128, rho * 128 : rho * 128 + 128]
        move[pl.ds(row + 2, 128, stride=8), :] = done[128:, rho * 128 : rho * 128 + 128]
    out_ref[...] = move[0:1024, :].astype(BF16)


def back_kernel(got_ref, first, twiddle, second, out_ref, send_ref, move, send):
    move[...] = got_ref[...].astype(F32)
    lines = jnp.concatenate([move[pl.ds(slot, 256, stride=4), :] for slot in range(4)], 1).astype(BF16)
    mixed = dot(first[...], twice(lines, 0))
    for row in range(2):
        at = row * 128
        real = mixed[:256, at : at + 128] - mixed[256:, 256 + at : 384 + at]
        imag = mixed[256:, at : at + 128] + mixed[:256, 256 + at : 384 + at]
        turned = jnp.concatenate(
            [real * twiddle[0] - imag * twiddle[1], real * twiddle[1] + imag * twiddle[0]], axis=1
        )
        done = dot(both(second, 1), parts(turned, 1), NT)
        for half in range(2):
            move[pl.ds(2 * half + row, 128, stride=4), :] = done[:, half * 128 : half * 128 + 128]
    for at in range(BLOCKS):
        piece = move[2 * at : 2 * at + 2, :]
        out_ref[:, at * 128 : at * 128 + 128] = piece
        send[2 * OWNER[at] : 2 * OWNER[at] + 2, :] = piece
    send_ref[...] = send[...].astype(BF16)


def gather_window(far, near, own, partner, cross, side):
    c1, c2 = math.cos(0.4 * math.pi), math.cos(0.8 * math.pi)
    s1, s2 = side * math.sin(0.4 * math.pi), side * math.sin(0.8 * math.pi)
    p1, m1, p2, m2 = near + partner, near - partner, far + cross, far - cross
    return [
        (own + p1 + p2, None),
        (own + c1 * p1 + c2 * p2, s1 * m1 + s2 * m2),
        (own + c2 * p1 + c1 * p2, s2 * m1 - s1 * m2),
    ]


def to_frequency(real, imag, right, side, left):
    if imag is None:
        lines = parts(real, 1)
        table = jnp.concatenate([right[0:128, :], right[0:128, :], right[256:384, :]], axis=0)
    else:
        lines = parts(jnp.concatenate([real, imag], axis=1), 1)
        table = both(right, 0)
    mixed = dot(lines, table)
    quarters = [
        (mixed[at * 128 : at * 128 + 128, :128], mixed[at * 128 : at * 128 + 128, 128:])
        for at in range(4)
    ]
    turned = []
    for at, (real, imag) in enumerate(cross_forward(quarters)):
        if at > 0:
            real, imag = turn_forward(real, imag, side[at - 1, 0], side[at - 1, 1])
        turned.append(jnp.concatenate([real, imag], axis=0))
    done = dot(both(left, 1), parts(jnp.concatenate(turned, axis=1), 0))
    return done[:128], done[128:]


def transfer_kernel(turn_ref, *refs):
    blocks = [ref[...].astype(F32) for ref in refs[:QUARTERS]]
    side, right, left, out_ref = refs[QUARTERS:]
    for phase in range(PHASES):
        real, imag = None, None
        for at, value in enumerate(blocks):
            place = 2 * (phase * QUARTERS + at)
            term = value * turn_ref[place] if phase else value
            real = term if real is None else real + term
            if phase:
                term = value * turn_ref[place + 1]
                imag = -term if imag is None else imag - term
        out_ref[phase, 0], out_ref[phase, 1] = to_frequency(
            real, imag, right.at[phase], side, left
        )


def conv_kernel(
    first, side_ref, far, near, own, partner, cross, transfer, side, right, left,
    back, window_back, sky_ref, resid_ref, base_ref, *out_refs,
):
    blocks = [ref[...].astype(F32) for ref in (far, near, own, partner, cross)]
    windows = gather_window(*blocks, side_ref[0])
    total = jnp.zeros((GV, 128), F32)
    for phase in range(PHASES):
        real, imag = to_frequency(*windows[phase], right.at[phase], side, left)
        trans_real, trans_imag = transfer[phase, 0], transfer[phase, 1]
        blur = jnp.concatenate(
            [real * trans_real - imag * trans_imag, real * trans_imag + imag * trans_real], axis=0
        )
        mixed = dot(both(back, 1), parts(blur, 0))
        quarters = []
        for at in range(4):
            real, imag = mixed[:128, at * 128 : at * 128 + 128], mixed[128:, at * 128 : at * 128 + 128]
            if at > 0:
                real, imag = turn_back(real, imag, side[at - 1, 0], side[at - 1, 1])
            quarters.append((real, imag))
        lines = [jnp.concatenate([real, imag], axis=1) for real, imag in cross_back(quarters)]
        high, low = window_back[phase, 0:256], window_back[phase, 256:512]
        table = jnp.concatenate([high, high, low], axis=0)
        total = total + dot(parts(jnp.concatenate(lines, axis=0), 1), table)
    resid = resid_ref[...].astype(F32)
    base = base_ref[...].astype(F32)
    sky = step(base, resid) if first else sky_ref[...]
    sky = step(sky, resid - total)
    if first:
        out_refs[0][...] = sky
        out_refs[1][...] = (sky - base).astype(BF16)
    else:
        out_refs[0][...] = sky.astype(BF16)


def step(sky, gradient):
    moved = sky + STEP_SIZE * gradient
    return moved - jnp.clip(moved, -THRESHOLD, THRESHOLD)


def last_kernel(got_ref, out_ref, move):
    move[...] = got_ref[...].astype(F32)
    for at in range(BLOCKS):
        out_ref[:, at * 128 : at * 128 + 128] = move[2 * OWNER[at] : 2 * OWNER[at] + 2, :]


def exchange(rows):
    blocks = rows.reshape(BLOCKS, rows.shape[0] // BLOCKS, 128)
    return lax.all_to_all(blocks, JOINT, 0, 0, tiled=True).reshape(rows.shape)


def halo(block, step):
    pairs = [(OWNER[at], OWNER[(at + step) % BLOCKS]) for at in range(BLOCKS)]
    return lax.ppermute(block, JOINT, pairs)


def swap_cores(block):
    return lax.ppermute(block, JOINT, [(OWNER[at], OWNER[at ^ 1]) for at in range(BLOCKS)])


def swap_edges(block):
    pairs = []
    for at in range(1, BLOCKS, 2):
        last, first = OWNER[at], OWNER[(at + 1) % BLOCKS]
        pairs += [(last, first), (first, last)]
    return lax.ppermute(block, JOINT, pairs)


def around_vis(value, step):
    return lax.ppermute(value, "vis", [(at, (at + step) % N_VIS) for at in range(N_VIS)])


def around_y(value, step):
    pairs = []
    for tile in range(N_TILE):
        at = tile // 2 % QUARTERS
        pairs.append((tile, tile + 2 * ((at + step) % QUARTERS - at)))
    return lax.ppermute(value, "tile", pairs)


def shards(
    model_image, psf, kernel_table, observed, visit_tile, visit_count, cell_offset, kernel_row
):
    at_vis = lax.axis_index("vis")
    at_y = lax.axis_index("tile") // 2 % QUARTERS
    tables = TABLES

    live = jnp.arange(CAP)[None, :] < visit_count[0][:, None]
    wide = observed[:, 0] * 65537.0
    high = wide - (wide - observed[:, 0])
    low = observed[:, 0] - high
    rows = [high[0], low[0], high[1], low[1], jnp.where(live, cell_offset[0, 0], 2 * UVT)]
    rows += [cell_offset[1, 0], kernel_row[0, 0], kernel_row[1, 0]]
    packed = jnp.stack([row.astype(BF16) for row in rows], axis=1).reshape(4, 32, CAP)
    tile_row = (visit_tile[0] % 4).astype(BF16).reshape(4, 4, 1)
    tile_row = jnp.pad(jnp.broadcast_to(tile_row, (4, 4, CAP)), ((0, 0), (0, 4), (0, 0)))
    packed = jnp.concatenate([packed, tile_row], axis=1)
    groups = [lax.dynamic_index_in_dim(packed, at_vis, 0, keepdims=False)]
    for hop in range(1, N_VIS):
        group = lax.dynamic_index_in_dim(packed, (at_vis + hop) % N_VIS, 0, keepdims=False)
        groups.append(around_vis(group, hop))

    send = call(
        row_kernel,
        [shape((8 * BLOCKS, 128), BF16)],
        model_image,
        psf,
        tables["point_right"],
        tables["half_twiddle"],
        tables["row_twiddle"],
        tables["point_left"],
        vmem=60,
        scratch=[pltpu.VMEM((512, 128), F32), pltpu.VMEM((8 * BLOCKS, 128), F32)],
        flops=2 * 3 * 256 * 256 * 1024,
    )[0]
    got = exchange(send)
    visit_rows = jnp.concatenate([group[32:36, 0] for group in groups]).astype(jnp.int32)
    taps = jnp.pad(kernel_table.astype(BF16).T, ((0, 8), (0, 0)))

    send, base, quarter = call(
        uv_kernel,
        [shape((4 * BLOCKS, 128), BF16), shape((GV, 128), BF16), shape((GV, 128), BF16)],
        visit_rows,
        got,
        *groups,
        taps,
        tables["point_right"],
        tables["point_back"],
        tables["lane_twiddle"],
        smem=(0,),
        scratch=[
            pltpu.VMEM((8 * BLOCKS, 128), F32),
            pltpu.VMEM((256, GV), BF16),
            pltpu.VMEM((256, GV), F32),
            pltpu.VMEM((GV, 128), F32),
            pltpu.VMEM((128, CAP), F32),
        ],
        flops=2 * 7 * 256 * 512 * 512,
    )
    got = exchange(send)
    transfer = call(
        transfer_kernel,
        [shape((PHASES, 2, 128, 4 * 128), F32)],
        lax.dynamic_index_in_dim(jnp.asarray(window_turns()), at_y, 0, keepdims=False),
        quarter,
        *[around_y(quarter, QUARTERS - hop) for hop in range(1, QUARTERS)],
        tables["side_twiddle"],
        tables["window_right"],
        tables["point_left"],
        smem=(0,),
        flops=2 * PHASES * 3 * 2 * 512 * 256 * 256,
    )[0]
    residual_image, send = call(
        back_kernel,
        [shape((2, GU), F32), shape((2 * BLOCKS, 128), BF16)],
        got,
        tables["back_first"],
        tables["back_twiddle"],
        tables["back_second"],
        scratch=[pltpu.VMEM((4 * BLOCKS, 128), F32), pltpu.VMEM((2 * BLOCKS, 128), F32)],
        flops=2 * 3 * 512 * 512 * 256,
    )

    resid = exchange(send)
    wide = base.astype(F32)
    change = (step(wide, resid.astype(F32)) - wide).astype(BF16)
    sky = wide
    side = jnp.where(lax.axis_index("tile") % 2 == 0, 1.0, -1.0).astype(F32).reshape(1)
    for turn in range(2):
        first = turn == 0
        if first:
            far, near, partner, cross = [halo(change, hop) for hop in (2, 1, -1, -2)]
        else:
            partner, near = swap_cores(change), swap_edges(change)
            far, cross = swap_edges(partner), swap_cores(near)
        outs = [shape((GV, 128), F32), shape((GV, 128), BF16)] if first else [shape((GV, 128), BF16)]
        got = call(
            functools.partial(conv_kernel, first),
            outs,
            jnp.ones((1,), F32) if first else side,
            far,
            near,
            change,
            partner,
            cross,
            transfer,
            tables["side_twiddle"],
            tables["window_right"],
            tables["point_left"],
            tables["point_back"],
            tables["window_back"],
            base if first else sky,
            resid,
            base,
            smem=(0,),
            flops=2 * PHASES * 3 * 4 * 512 * 256 * 256,
        )
        if first:
            sky, change = got
    got = exchange(got[0])
    model_next = call(
        last_kernel, [shape((2, GU), F32)], got, scratch=[pltpu.VMEM((2 * BLOCKS, 128), F32)]
    )[0]
    return (model_next, residual_image)


def solution(mesh):
    placed = (
        P(("tile", "vis"), None),
        P(("tile", "vis"), None),
        P(),
        P(None, "vis", "tile", None),
        P("vis", "tile"),
        P("vis", "tile"),
        P(None, "vis", "tile", None),
        P(None, "vis", "tile", None),
    )
    return jax.shard_map(
        shards,
        mesh=mesh,
        in_specs=placed,
        out_specs=(P(("tile", "vis"), None), P(("tile", "vis"), None)),
        check_vma=False,
    )
```

```python
import functools
import math

import jax
import jax.numpy as jnp
import numpy as np
from jax import lax
from jax.experimental import pallas as pl
from jax.experimental.pallas import tpu as pltpu
from jax.sharding import PartitionSpec as P

GU = 32768
GV = 512
UVT = 128
CAP = 256
N_TILE = 64
N_VIS = 4
BLOCKS = N_TILE * N_VIS
WIDTH = GU // BLOCKS
HALO = 640
PHASES = 3
QUARTERS = 4
STEP_SIZE = 0.5
THRESHOLD = 0.05
JOINT = ("tile", "vis")
F32 = jnp.float32
BF16 = jnp.bfloat16
NN = (((1,), (0,)), ((), ()))
NT = (((1,), (1,)), ((), ()))
TN = (((0,), (0,)), ((), ()))
MIB = 1024 * 1024


def angles(left, right, length):
    return 2.0 * math.pi / length * ((np.asarray(left)[:, None] * np.asarray(right)[None, :]) % length)


def split_table(table, axis):
    table = np.asarray(table, np.float32)
    high = table.astype(jnp.bfloat16)
    low = (table - high.astype(np.float32)).astype(jnp.bfloat16)
    return np.concatenate([high, low], axis)


def block_owner():
    owner = []
    for run in range(16):
        x, y = run // 4, run % 4
        y = y if x % 2 == 0 else 3 - y
        for spot in range(8):
            z = spot if run % 2 == 0 else 7 - spot
            for core in range(2):
                owner.append((((x * 2 + z // 4) * 4 + y) * 2 + core) * 4 + z % 4)
    return owner


def build_tables():
    tables = {}
    scale = 1.0 / math.sqrt(GV * GU)
    first = angles(np.arange(256), np.arange(256), 256)
    second = angles(np.arange(128), np.arange(128), 128)
    cosine, sine = np.cos(second), np.sin(second)
    twiddle = angles(np.arange(128), np.arange(256), GU)
    tables["row_twiddle"] = (np.stack([np.cos(twiddle), -np.sin(twiddle)]) * scale).astype(np.float32)
    half = angles([1], np.arange(128), 256)
    tables["half_twiddle"] = np.concatenate([np.cos(half), np.sin(half)]).astype(np.float32)
    tables["back_first"] = split_table(np.concatenate([np.cos(first), np.sin(first)], 0), 1)
    tables["back_twiddle"] = np.stack([np.cos(twiddle.T), np.sin(twiddle.T)]).astype(np.float32)
    tables["back_second"] = split_table(np.concatenate([cosine, -sine], 1) * scale, 1)
    block = np.block([[cosine, -sine], [sine, cosine]])
    tables["point_right"] = split_table(block, 0)
    tables["point_left"] = split_table(block.T, 1)
    tables["point_back"] = split_table(block, 1)
    quarter = angles(np.arange(4), np.arange(128), GV)
    tables["lane_twiddle"] = np.stack([np.cos(quarter), np.sin(quarter)], 1).astype(np.float32)
    rows = np.stack([np.cos(quarter[1:]), np.sin(quarter[1:])], 1)[:, :, :, None]
    tables["side_twiddle"] = np.broadcast_to(rows, (3, 2, 128, 128)).astype(np.float32)
    right, back = [], []
    for phase in range(PHASES):
        turn = angles(np.arange(128), 5 * np.arange(128) + phase, HALO)
        turn = np.block([[np.cos(turn), -np.sin(turn)], [np.sin(turn), np.cos(turn)]])
        right.append(split_table(turn, 0))
        share = (1.0 if phase == 0 else 2.0) / (GV * HALO)
        turn = angles(5 * np.arange(128) + phase, np.arange(128), HALO)
        back.append(split_table(np.concatenate([np.cos(turn), -np.sin(turn)], 0) * share, 0))
    tables["window_right"] = np.stack(right)
    tables["window_back"] = np.stack(back)
    return tables


TABLES = build_tables()
OWNER = block_owner()


def window_turns():
    place = np.array([3, 4, 0, 1])
    out = np.zeros((QUARTERS, PHASES, QUARTERS, 2), np.float32)
    for at in range(QUARTERS):
        for phase in range(PHASES):
            for block in range(QUARTERS):
                turn = 2.0 * math.pi * (place[(at + block) % QUARTERS] * phase % 5) / 5.0
                out[at, phase, block] = (math.cos(turn), math.sin(turn))
    return out.reshape(QUARTERS, -1)


def dot(left, right, dims=NN):
    return lax.dot_general(left, right, dims, preferred_element_type=F32)


def parts(value, axis):
    high = value.astype(BF16)
    low = (value - high.astype(F32)).astype(BF16)
    return jnp.concatenate([high, low, high], axis=axis)


def both(table, axis):
    high, low = jnp.split(table[...], 2, axis=axis)
    return jnp.concatenate([high, high, low], axis=axis)


def twice(value, axis):
    return jnp.concatenate([value, value], axis=axis)


def call(kernel, outs, *args, smem=(), scratch=(), flops=0, vmem=32):
    specs = [
        pl.BlockSpec(memory_space=pltpu.SMEM if at in smem else pltpu.VMEM) for at in range(len(args))
    ]
    size = sum(int(np.prod(a.shape)) * a.dtype.itemsize for a in args)
    size += sum(int(np.prod(o.shape)) * o.dtype.itemsize for o in outs)
    return pl.pallas_call(
        kernel,
        out_shape=outs,
        in_specs=specs,
        out_specs=[pl.BlockSpec(memory_space=pltpu.VMEM)] * len(outs),
        scratch_shapes=list(scratch),
        compiler_params=pltpu.CompilerParams(vmem_limit_bytes=vmem * MIB),
        cost_estimate=pl.CostEstimate(flops=flops, bytes_accessed=size, transcendentals=0),
    )(*args)


def shape(dims, dtype):
    return jax.ShapeDtypeStruct(dims, dtype)


def cross_forward(blocks):
    (r0, i0), (r1, i1), (r2, i2), (r3, i3) = blocks
    ar, ai, br, bi = r0 + r2, i0 + i2, r0 - r2, i0 - i2
    cr, ci, dr, di = r1 + r3, i1 + i3, r1 - r3, i1 - i3
    return [(ar + cr, ai + ci), (br + di, bi - dr), (ar - cr, ai - ci), (br - di, bi + dr)]


def cross_back(blocks):
    (r0, i0), (r1, i1), (r2, i2), (r3, i3) = blocks
    ar, ai, br, bi = r0 + r2, i0 + i2, r0 - r2, i0 - i2
    cr, ci, dr, di = r1 + r3, i1 + i3, r1 - r3, i1 - i3
    return [(ar + cr, ai + ci), (br - di, bi + dr), (ar - cr, ai - ci), (br + di, bi - dr)]


def turn_forward(real, imag, cosine, sine):
    return real * cosine + imag * sine, imag * cosine - real * sine


def turn_back(real, imag, cosine, sine):
    return real * cosine - imag * sine, imag * cosine + real * sine


def row_kernel(sky_ref, psf_ref, right, half_turn, twiddle, left, out_ref, lines, send):
    for at in range(BLOCKS):
        piece = sky_ref[:, at * 128 : at * 128 + 128]
        lines[2 * at : 2 * at + 2, :] = piece
        row = 8 * OWNER[at] + 4
        send[row : row + 2, :] = piece
    for at in range(QUARTERS):
        piece = psf_ref[:, at * 128 : at * 128 + 128]
        for device in range(BLOCKS):
            if device // 8 % QUARTERS == at:
                send[8 * device + 6 : 8 * device + 8, :] = piece
    pieces = [
        lines[pl.ds(2 * odd + row, 128, stride=4), :] for row in range(2) for odd in range(2)
    ]
    high, low = right[0:128, :], right[256:384, :]
    mixed = dot(parts(jnp.concatenate(pieces, 1), 0), jnp.concatenate([high, high, low], 0), TN)
    for row in range(2):
        even = mixed[row * 256 : row * 256 + 128]
        odd = mixed[row * 256 + 128 : row * 256 + 256]
        odd_real, odd_imag = turn_forward(odd[:, :128], odd[:, 128:], half_turn[0:1], half_turn[1:2])
        real = jnp.concatenate([even[:, :128] + odd_real, even[:, :128] - odd_real], axis=1)
        imag = jnp.concatenate([even[:, 128:] + odd_imag, even[:, 128:] - odd_imag], axis=1)
        turned = jnp.concatenate(
            [real * twiddle[0] - imag * twiddle[1], real * twiddle[1] + imag * twiddle[0]], axis=0
        )
        done = dot(both(left, 1), parts(turned, 0))
        for half in range(2):
            send[pl.ds(8 * half + row, 128, stride=16), :] = done[:128, half * 128 : half * 128 + 128]
            send[pl.ds(8 * half + 2 + row, 128, stride=16), :] = done[128:, half * 128 : half * 128 + 128]
    out_ref[...] = send[...].astype(BF16)


def spread_taps(taps_table, offset, row, place):
    index = jnp.broadcast_to(row.astype(jnp.int32), (8, CAP))
    taps = jnp.concatenate(
        [
            jnp.take_along_axis(taps_table, index[:, at : at + 128], axis=1, mode="promise_in_bounds")
            for at in range(0, CAP, 128)
        ],
        axis=1,
    )
    turn = (place[0:8].astype(jnp.int32) - offset.astype(jnp.int32)) & 7
    turned = jnp.zeros((8, CAP), F32)
    for shift in range(8):
        turned = jnp.where(turn == shift, taps[shift : shift + 1, :], turned)
    within = place - offset
    keep = jnp.abs(within - 3.5) < 4.0
    return jnp.where(keep, jnp.concatenate([turned] * (UVT // 8), axis=0), 0.0)


def uv_kernel(
    tile_ref, got_ref, group_0, group_1, group_2, group_3, taps_ref, right, back, twiddle,
    out_ref, base_ref, psf_ref, move, grid, resid, side, visits,
):
    for at, group in enumerate((group_0, group_1, group_2, group_3)):
        visits[32 * at : 32 * at + 32, :] = group[...].astype(F32)[0:32]
    move[...] = got_ref[...].astype(F32)
    for slot, ref in ((4, base_ref), (6, psf_ref)):
        for row in range(2):
            side[pl.ds(row, 256, stride=2), :] = move[pl.ds(slot + row, 256, stride=8), :]
        ref[...] = side[...].astype(BF16)
    lines = []
    for rho in range(4):
        row = 8 * (rho // 2) + rho % 2
        lines.append(
            jnp.concatenate(
                [move[pl.ds(row, 128, stride=16), :], move[pl.ds(row + 2, 128, stride=16), :]], 0
            )
        )
    lines = jnp.concatenate(lines, axis=1).astype(BF16)
    mixed = dot(twice(lines, 0), right[...], TN)
    blocks = []
    for rho in range(4):
        real, imag = mixed[rho * 128 : rho * 128 + 128, :128], mixed[rho * 128 : rho * 128 + 128, 128:]
        if rho > 0:
            real, imag = turn_forward(real, imag, twiddle[rho, 0:1], twiddle[rho, 1:2])
        blocks.append((real, imag))
    for at, (real, imag) in enumerate(cross_forward(blocks)):
        grid[0:128, at * 128 : at * 128 + 128] = real.astype(BF16)
        grid[128:256, at * 128 : at * 128 + 128] = imag.astype(BF16)
    resid[...] = jnp.zeros_like(resid)
    taps_table = taps_ref[...].astype(F32)[0:8]
    place = lax.broadcasted_iota(jnp.int32, (UVT, CAP), 0).astype(F32)

    def some(group, carry):
        for side in range(8):
            at = 8 * group + side
            start = pl.multiple_of(tile_ref[at] * UVT, UVT)
            entry = visits[pl.ds(pl.multiple_of(8 * at, 8), 8), :]
            weight_row = spread_taps(taps_table, entry[4:5], entry[6:7], place).astype(BF16)
            weight_col = spread_taps(taps_table, entry[5:6], entry[7:8], place)
            partial = dot(grid[:, pl.ds(start, UVT)], weight_row)
            model_real = jnp.sum(partial[:UVT] * weight_col, axis=0, keepdims=True)
            model_imag = jnp.sum(partial[UVT:] * weight_col, axis=0, keepdims=True)
            real = entry[0:1] + entry[1:2] - model_real
            imag = entry[2:3] + entry[3:4] - model_imag
            spread = jnp.concatenate([real * weight_col, imag * weight_col], axis=0).astype(BF16)
            resid[:, pl.ds(start, UVT)] += dot(spread, weight_row, NT)
        return carry

    lax.fori_loop(0, 2, some, 0)
    blocks = [
        (resid[0:128, at * 128 : at * 128 + 128], resid[128:256, at * 128 : at * 128 + 128])
        for at in range(4)
    ]
    turned = []
    for rho, (real, imag) in enumerate(cross_back(blocks)):
        if rho > 0:
            real, imag = turn_back(real, imag, twiddle[rho, 0:1], twiddle[rho, 1:2])
        turned.append(jnp.concatenate([real, imag], axis=1))
    done = dot(both(back, 1), parts(jnp.concatenate(turned, axis=0), 1), NT)
    for rho in range(4):
        row = 4 * (rho // 2) + rho % 2
        move[pl.ds(row, 128, stride=8), :] = done[:128, rho * 128 : rho * 128 + 128]
        move[pl.ds(row + 2, 128, stride=8), :] = done[128:, rho * 128 : rho * 128 + 128]
    out_ref[...] = move[0:1024, :].astype(BF16)


def back_kernel(got_ref, first, twiddle, second, out_ref, send_ref, move, send):
    move[...] = got_ref[...].astype(F32)
    lines = jnp.concatenate([move[pl.ds(slot, 256, stride=4), :] for slot in range(4)], 1).astype(BF16)
    mixed = dot(first[...], twice(lines, 0))
    for row in range(2):
        at = row * 128
        real = mixed[:256, at : at + 128] - mixed[256:, 256 + at : 384 + at]
        imag = mixed[256:, at : at + 128] + mixed[:256, 256 + at : 384 + at]
        turned = jnp.concatenate(
            [real * twiddle[0] - imag * twiddle[1], real * twiddle[1] + imag * twiddle[0]], axis=1
        )
        done = dot(both(second, 1), parts(turned, 1), NT)
        for half in range(2):
            move[pl.ds(2 * half + row, 128, stride=4), :] = done[:, half * 128 : half * 128 + 128]
    for at in range(BLOCKS):
        piece = move[2 * at : 2 * at + 2, :]
        out_ref[:, at * 128 : at * 128 + 128] = piece
        send[2 * OWNER[at] : 2 * OWNER[at] + 2, :] = piece
    send_ref[...] = send[...].astype(BF16)


def gather_window(far, near, own, partner, cross, side):
    c1, c2 = math.cos(0.4 * math.pi), math.cos(0.8 * math.pi)
    s1, s2 = side * math.sin(0.4 * math.pi), side * math.sin(0.8 * math.pi)
    p1, m1, p2, m2 = near + partner, near - partner, far + cross, far - cross
    return [
        (own + p1 + p2, None),
        (own + c1 * p1 + c2 * p2, s1 * m1 + s2 * m2),
        (own + c2 * p1 + c1 * p2, s2 * m1 - s1 * m2),
    ]


def to_frequency(real, imag, right, side, left):
    if imag is None:
        lines = parts(real, 1)
        table = jnp.concatenate([right[0:128, :], right[0:128, :], right[256:384, :]], axis=0)
    else:
        lines = parts(jnp.concatenate([real, imag], axis=1), 1)
        table = both(right, 0)
    mixed = dot(lines, table)
    quarters = [
        (mixed[at * 128 : at * 128 + 128, :128], mixed[at * 128 : at * 128 + 128, 128:])
        for at in range(4)
    ]
    turned = []
    for at, (real, imag) in enumerate(cross_forward(quarters)):
        if at > 0:
            real, imag = turn_forward(real, imag, side[at - 1, 0], side[at - 1, 1])
        turned.append(jnp.concatenate([real, imag], axis=0))
    done = dot(both(left, 1), parts(jnp.concatenate(turned, axis=1), 0))
    return done[:128], done[128:]


def transfer_kernel(at_ref, turn_ref, *refs):
    base = at_ref[0] * (2 * PHASES * QUARTERS)
    blocks = [ref[...].astype(F32) for ref in refs[:QUARTERS]]
    side, right, left, out_ref = refs[QUARTERS:]
    for phase in range(PHASES):
        real, imag = None, None
        for at, value in enumerate(blocks):
            place = base + 2 * (phase * QUARTERS + at)
            term = value * turn_ref[place] if phase else value
            real = term if real is None else real + term
            if phase:
                term = value * turn_ref[place + 1]
                imag = -term if imag is None else imag - term
        out_ref[phase, 0], out_ref[phase, 1] = to_frequency(
            real, imag, right.at[phase], side, left
        )


def conv_kernel(
    first, side_ref, far, near, own, partner, cross, transfer, side, right, left,
    back, window_back, sky_ref, resid_ref, base_ref, *out_refs,
):
    blocks = [ref[...].astype(F32) for ref in (far, near, own, partner, cross)]
    windows = gather_window(*blocks, side_ref[0])
    total = jnp.zeros((GV, 128), F32)
    for phase in range(PHASES):
        real, imag = to_frequency(*windows[phase], right.at[phase], side, left)
        trans_real, trans_imag = transfer[phase, 0], transfer[phase, 1]
        blur = jnp.concatenate(
            [real * trans_real - imag * trans_imag, real * trans_imag + imag * trans_real], axis=0
        )
        mixed = dot(both(back, 1), parts(blur, 0))
        quarters = []
        for at in range(4):
            real, imag = mixed[:128, at * 128 : at * 128 + 128], mixed[128:, at * 128 : at * 128 + 128]
            if at > 0:
                real, imag = turn_back(real, imag, side[at - 1, 0], side[at - 1, 1])
            quarters.append((real, imag))
        lines = [jnp.concatenate([real, imag], axis=1) for real, imag in cross_back(quarters)]
        high, low = window_back[phase, 0:256], window_back[phase, 256:512]
        table = jnp.concatenate([high, high, low], axis=0)
        total = total + dot(parts(jnp.concatenate(lines, axis=0), 1), table)
    resid = resid_ref[...].astype(F32)
    base = base_ref[...].astype(F32)
    sky = step(base, resid) if first else sky_ref[...]
    sky = step(sky, resid - total)
    if first:
        out_refs[0][...] = sky
        out_refs[1][...] = (sky - base).astype(BF16)
    else:
        out_refs[0][...] = sky.astype(BF16)


def step(sky, gradient):
    moved = sky + STEP_SIZE * gradient
    return moved - jnp.clip(moved, -THRESHOLD, THRESHOLD)


def last_kernel(got_ref, out_ref, move):
    move[...] = got_ref[...].astype(F32)
    for at in range(BLOCKS):
        out_ref[:, at * 128 : at * 128 + 128] = move[2 * OWNER[at] : 2 * OWNER[at] + 2, :]


def exchange(rows):
    blocks = rows.reshape(BLOCKS, rows.shape[0] // BLOCKS, 128)
    return lax.all_to_all(blocks, JOINT, 0, 0, tiled=True).reshape(rows.shape)


def halo(block, step):
    pairs = [(OWNER[at], OWNER[(at + step) % BLOCKS]) for at in range(BLOCKS)]
    return lax.ppermute(block, JOINT, pairs)


def swap_cores(block):
    return lax.ppermute(block, JOINT, [(OWNER[at], OWNER[at ^ 1]) for at in range(BLOCKS)])


def swap_edges(block):
    pairs = []
    for at in range(1, BLOCKS, 2):
        last, first = OWNER[at], OWNER[(at + 1) % BLOCKS]
        pairs += [(last, first), (first, last)]
    return lax.ppermute(block, JOINT, pairs)


def around_vis(value, step):
    return lax.ppermute(value, "vis", [(at, (at + step) % N_VIS) for at in range(N_VIS)])


def around_y(value, step):
    pairs = []
    for tile in range(N_TILE):
        at = tile // 2 % QUARTERS
        pairs.append((tile, tile + 2 * ((at + step) % QUARTERS - at)))
    return lax.ppermute(value, "tile", pairs)


def shards(
    model_image, psf, kernel_table, observed, visit_tile, visit_count, cell_offset, kernel_row
):
    at_vis = lax.axis_index("vis")
    at_y = lax.axis_index("tile") // 2 % QUARTERS
    tables = TABLES

    live = jnp.arange(CAP)[None, :] < visit_count[0][:, None]
    wide = observed[:, 0] * 65537.0
    high = wide - (wide - observed[:, 0])
    low = observed[:, 0] - high
    rows = [high[0], low[0], high[1], low[1], jnp.where(live, cell_offset[0, 0], 2 * UVT)]
    rows += [cell_offset[1, 0], kernel_row[0, 0], kernel_row[1, 0]]
    packed = jnp.stack([row.astype(BF16) for row in rows], axis=1).reshape(4, 32, CAP)
    tile_row = (visit_tile[0] % 4).astype(BF16).reshape(4, 4, 1)
    tile_row = jnp.pad(jnp.broadcast_to(tile_row, (4, 4, CAP)), ((0, 0), (0, 4), (0, 0)))
    packed = jnp.concatenate([packed, tile_row], axis=1)
    groups = [lax.dynamic_index_in_dim(packed, at_vis, 0, keepdims=False)]
    for hop in range(1, N_VIS):
        group = lax.dynamic_index_in_dim(packed, (at_vis + hop) % N_VIS, 0, keepdims=False)
        groups.append(around_vis(group, hop))

    send = call(
        row_kernel,
        [shape((8 * BLOCKS, 128), BF16)],
        model_image,
        psf,
        tables["point_right"],
        tables["half_twiddle"],
        tables["row_twiddle"],
        tables["point_left"],
        vmem=60,
        scratch=[pltpu.VMEM((512, 128), F32), pltpu.VMEM((8 * BLOCKS, 128), F32)],
        flops=2 * 3 * 256 * 256 * 1024,
    )[0]
    got = exchange(send)
    visit_rows = jnp.concatenate([group[32:36, 0] for group in groups]).astype(jnp.int32)
    taps = jnp.pad(kernel_table.astype(BF16).T, ((0, 8), (0, 0)))

    send, base, quarter = call(
        uv_kernel,
        [shape((4 * BLOCKS, 128), BF16), shape((GV, 128), BF16), shape((GV, 128), BF16)],
        visit_rows,
        got,
        *groups,
        taps,
        tables["point_right"],
        tables["point_back"],
        tables["lane_twiddle"],
        smem=(0,),
        scratch=[
            pltpu.VMEM((8 * BLOCKS, 128), F32),
            pltpu.VMEM((256, GV), BF16),
            pltpu.VMEM((256, GV), F32),
            pltpu.VMEM((GV, 128), F32),
            pltpu.VMEM((128, CAP), F32),
        ],
        flops=2 * 7 * 256 * 512 * 512,
    )
    got = exchange(send)
    transfer = call(
        transfer_kernel,
        [shape((PHASES, 2, 128, 4 * 128), F32)],
        at_y.astype(jnp.int32).reshape(1),
        jnp.asarray(window_turns().reshape(-1)),
        quarter,
        *[around_y(quarter, QUARTERS - hop) for hop in range(1, QUARTERS)],
        tables["side_twiddle"],
        tables["window_right"],
        tables["point_left"],
        smem=(0, 1),
        flops=2 * PHASES * 3 * 2 * 512 * 256 * 256,
    )[0]
    residual_image, send = call(
        back_kernel,
        [shape((2, GU), F32), shape((2 * BLOCKS, 128), BF16)],
        got,
        tables["back_first"],
        tables["back_twiddle"],
        tables["back_second"],
        scratch=[pltpu.VMEM((4 * BLOCKS, 128), F32), pltpu.VMEM((2 * BLOCKS, 128), F32)],
        flops=2 * 3 * 512 * 512 * 256,
    )

    resid = exchange(send)
    wide = base.astype(F32)
    change = (step(wide, resid.astype(F32)) - wide).astype(BF16)
    sky = wide
    side = jnp.where(lax.axis_index("tile") % 2 == 0, 1.0, -1.0).astype(F32).reshape(1)
    for turn in range(2):
        first = turn == 0
        if first:
            far, near, partner, cross = [halo(change, hop) for hop in (2, 1, -1, -2)]
        else:
            partner, near = swap_cores(change), swap_edges(change)
            far, cross = swap_edges(partner), swap_cores(near)
        outs = [shape((GV, 128), F32), shape((GV, 128), BF16)] if first else [shape((GV, 128), BF16)]
        got = call(
            functools.partial(conv_kernel, first),
            outs,
            jnp.ones((1,), F32) if first else side,
            far,
            near,
            change,
            partner,
            cross,
            transfer,
            tables["side_twiddle"],
            tables["window_right"],
            tables["point_left"],
            tables["point_back"],
            tables["window_back"],
            base if first else sky,
            resid,
            base,
            smem=(0,),
            flops=2 * PHASES * 3 * 4 * 512 * 256 * 256,
        )
        if first:
            sky, change = got
    got = exchange(got[0])
    model_next = call(
        last_kernel, [shape((2, GU), F32)], got, scratch=[pltpu.VMEM((2 * BLOCKS, 128), F32)]
    )[0]
    return (model_next, residual_image)


def solution(mesh):
    placed = (
        P(("tile", "vis"), None),
        P(("tile", "vis"), None),
        P(),
        P(None, "vis", "tile", None),
        P("vis", "tile"),
        P("vis", "tile"),
        P(None, "vis", "tile", None),
        P(None, "vis", "tile", None),
    )
    return jax.shard_map(
        shards,
        mesh=mesh,
        in_specs=placed,
        out_specs=(P(("tile", "vis"), None), P(("tile", "vis"), None)),
        check_vma=False,
    )
```
